512 devices in a mesh: tok: 32 (over z, x), cen: 16 (over y, core).
Axes of the slice: x: 4, y: 8, z: 8, core: 2. Of those that a mesh axis runs over, the one named last changes fastest.
Arguments:
- tokens: bfloat16 [4096, 128], P('tok'), may hold values from -128 to 128
- nearest: int32 [4096], P('tok'), may hold values from 0 to 524287
- centroids: bfloat16 [524288, 128], P(('tok', 'cen')), may hold values from -32 to 32
- log_prior: float32 [524288], P(('tok', 'cen')), may hold values from -1.2 to 3.4
Outputs:
- updated: bfloat16 [524288, 128], P(('tok', 'cen'))
- log_norm: float32 [4096], P('tok')
- residual: bfloat16 [4096, 128], P(('tok', 'cen'))
The draws below stay inside these ranges and needn't reach their ends.
All inputs are finite; a program needn't handle non-finite values.
Results may differ from the reference program's by a relative error of at most 0.005.
Values may be sent and summed in bfloat16 or wider, within the bound.
A program may use at most 128 MiB of HBM per device.

```python
import math
import jax
import jax.numpy as jnp
from jax import lax

D = 128
CEN_DEV = 1024
TOKENS = 4096
CENTROIDS = 524288
N_CEN = 16


def draw_centroids(key, part):
    key = jax.random.fold_in(key, 11)
    values = jnp.clip(jax.random.normal(key, (CENTROIDS, D), jnp.float32), -6.0, 6.0)
    return values.astype(jnp.bfloat16)


def draw_tokens(key, part):
    key = jax.random.fold_in(key, 23)
    first_key = jax.random.fold_in(key, 0)
    values = jnp.clip(jax.random.normal(first_key, (TOKENS, D), jnp.float32), -6.0, 6.0)
    return values.astype(jnp.bfloat16)


def draw_log_prior(key, part):
    key = jax.random.fold_in(key, 37)
    frac = jnp.arange(CENTROIDS).astype(jnp.float32) / (CENTROIDS - 1)
    noise = jax.random.uniform(key, (CENTROIDS,), jnp.float32, -1.2, 1.2)
    return jnp.log1p(2.0 * frac) + noise


def set_ends(result, key, smallest, top_value):
    index_at = [jax.random.randint(jax.random.fold_in(key, axis), (), 0, length) for axis, length in enumerate(result.shape)]
    widest = result.shape.index(max(result.shape))
    neighbour = index_at[:widest] + [(index_at[widest] + 1) % result.shape[widest]] + index_at[widest + 1:]
    return result.at[tuple(index_at)].set(smallest).at[tuple(neighbour)].set(top_value)


def setup_inputs(seed: int = 0) -> dict:
    key_list = jax.random.split(jax.random.key(seed), 5)
    return {
        "tokens": draw_tokens(jax.random.fold_in(key_list[4], 71), 0),
        "nearest": set_ends(jax.random.randint(key_list[1], (TOKENS,), 0, CENTROIDS), jax.random.fold_in(key_list[1], 1), 0, CENTROIDS - 1).astype(jnp.int32),
        "centroids": draw_centroids(jax.random.fold_in(key_list[4], 71), 0),
        "log_prior": draw_log_prior(jax.random.fold_in(key_list[4], 71), 0),
    }


def block_scores(tokens, cblock, pblock):
    scale = 1.0 / math.sqrt(D)
    return jnp.dot(tokens, cblock.T, preferred_element_type=jnp.float32) * scale + pblock[None, :]

def reference(tokens, nearest, centroids, log_prior):
    width = CEN_DEV * N_CEN
    count = CENTROIDS // width
    cblocks = centroids.reshape(count, width, D)
    pblocks = log_prior.reshape(count, width)

    def first_pass(carry, inputs):
        run_max, run_sum = carry
        scores = block_scores(tokens, inputs[0], inputs[1])
        newest = jnp.maximum(run_max, lax.optimization_barrier(jnp.max(scores, axis=1)))
        run_sum = run_sum * jnp.exp(run_max - newest) + lax.optimization_barrier(jnp.sum(jnp.exp(scores - newest[:, None]), axis=1))
        return ((newest, run_sum), None)
    start = (jnp.full((TOKENS,), -jnp.inf, jnp.float32), jnp.zeros((TOKENS,), jnp.float32))
    (run_max, run_sum), unused = lax.scan(first_pass, start, (cblocks, pblocks))
    log_norm = run_max + jnp.log(run_sum)

    def second_pass(inputs):
        scores = block_scores(tokens, inputs[0], inputs[1])
        weight = jnp.exp(scores - log_norm[:, None]).astype(jnp.bfloat16)
        sums = jnp.dot(weight.T, tokens, preferred_element_type=jnp.float32)
        mass = lax.optimization_barrier(jnp.sum(weight.astype(jnp.float32), axis=0))
        return (sums / mass[:, None]).astype(jnp.bfloat16)
    updated = lax.map(second_pass, (cblocks, pblocks)).reshape(CENTROIDS, D)
    picked = centroids[nearest]
    residual = (tokens.astype(jnp.float32) - picked.astype(jnp.float32)).astype(jnp.bfloat16)
    return (updated, log_norm, residual)
```

```python
import functools
import math

import jax
import jax.numpy as jnp
from jax import lax
from jax.experimental import pallas as pl
from jax.experimental.pallas import tpu as pltpu
from jax.sharding import PartitionSpec as P

MESH = pl.DeviceIdType.MESH
NX, NY, NZ = 4, 8, 8
N_TOK, N_CEN = 32, 16
ROWS = 128
WIDTH = 128
LOCAL = 1024
CHUNK = 256
LN2 = math.log(2.0)


def ring(s):
    half = (s + 1) // 2
    return half * (2 * (s % 2) - 1)


def loop(lo, hi, body):
    def step(i, carry):
        body(i)
        return carry

    lax.fori_loop(lo, hi, step, 0)


def split3(v):
    hi = v.astype(jnp.bfloat16).astype(jnp.float32)
    mid = (v - hi).astype(jnp.bfloat16).astype(jnp.float32)
    return hi, mid, v - hi - mid


def kernel(
    tok_ref, ids_ref, cen_ref, lp_ref, upd_ref, norm_ref, res_ref,
    tok_all, ids_all, cen2, cen_aug, e_ref, g_ref, m_ref, l_send, l_cen, l_tok, l_all, flat,
    cols, py, pr, r_send, r_recv, tok_f32,
    tok_s, tok_r, fwd_s, fwd_r, ids_s, ids_r, cen_s, cen_r,
    lc_s, lc_r, lt_s, lt_r, la_s, la_r, py_s, py_r, rt_s, rt_r,
):
    t = lax.axis_index("tok")
    n = lax.axis_index("cen")
    x, z = t % NX, t // NX
    y, c = n // 2, n % 2
    sib = (t, y * 2 + 1 - c)
    unit = math.log2(math.e) / math.sqrt(WIDTH)

    def copy(src, dst, send, recv, dev):
        return pltpu.make_async_remote_copy(
            src_ref=src, dst_ref=dst, send_sem=send, recv_sem=recv, device_id=dev, device_id_type=MESH
        )

    barrier = pltpu.get_barrier_semaphore()

    def greet_tok(r):
        pl.semaphore_signal(barrier, inc=1, device_id=((t + r) % N_TOK, n), device_id_type=MESH)

    def greet_cen(r):
        pl.semaphore_signal(barrier, inc=1, device_id=(t, (n + r) % N_CEN), device_id_type=MESH)

    loop(1, N_TOK, greet_tok)
    loop(1, N_CEN, greet_cen)

    tok_all[pl.ds(t, 1)] = tok_ref[...][None]
    tok_f32[...] = tok_ref[...].astype(jnp.float32)
    ids_all[pl.ds(t, 1)] = ids_ref[...][None]
    cen2[pl.ds(c, 1)] = cen_ref[...][None]
    lane = lax.broadcasted_iota(jnp.int32, (ROWS, WIDTH), 1)
    lp_cols = jnp.transpose(lp_ref[...] * math.sqrt(WIDTH))
    for a in range(LOCAL // ROWS):
        hi, mid, low = split3(lp_cols[:, a : a + 1])
        extra = jnp.where(lane == 0, hi, jnp.where(lane == 1, mid, jnp.where(lane == 2, low, 0.0)))
        cen_aug[a * ROWS : (a + 1) * ROWS, WIDTH:] = extra.astype(jnp.bfloat16)
    cen_aug[:, :WIDTH] = cen_ref[...]

    pl.semaphore_wait(barrier, N_TOK - 1 + N_CEN - 1)

    def ids_copy(r):
        return copy(ids_ref, ids_all.at[t], ids_s.at[r], ids_r.at[r], ((t + r) % N_TOK, n))

    def cen_copy():
        return copy(cen_ref, cen2.at[c], cen_s, cen_r, sib)

    def tok_copy(s, q):
        xr = (c + s) % 2 + 2 * q
        dev = (((z - ring(s) + NZ) % NZ) * NX + (x - xr + NX) % NX, n)
        return copy(tok_ref, tok_all.at[t], tok_s.at[s, q], tok_r.at[s, q], dev)

    def fwd_copy(s, q):
        xr = (c + s) % 2 + 2 * q
        block = ((z + ring(s) + NZ) % NZ) * NX + (x + xr) % NX
        return copy(tok_all.at[block], tok_all.at[block], fwd_s.at[s, q], fwd_r.at[s, q], sib)

    def mine(s, q, core):
        return (s * 4 + q * 2 + (core + s) % 2) > 0

    loop(1, N_TOK, lambda r: ids_copy(r).start())
    cen_copy().start()

    def send_tokens(s):
        for q in range(2):
            @pl.when(mine(s, q, c))
            def _():
                tok_copy(s, q).start()

    loop(0, NZ, send_tokens)

    def receive(s):
        for q in range(2):
            @pl.when(mine(s, q, c))
            def _():
                tok_copy(s, q).wait_recv()
                fwd_copy(s, q).start()

    ones = jnp.where(lax.broadcasted_iota(jnp.int32, (CHUNK, WIDTH), 1) < 3, 1.0, 0.0).astype(jnp.bfloat16)

    def lc_copy(ch):
        return copy(l_send.at[ch], l_cen.at[n], lc_s.at[ch], lc_r.at[n], (t, ch))

    def score(s):
        for q in range(2):
            @pl.when(mine(s, q, 1 - c))
            def _():
                fwd_copy(s, q).wait_recv()
        zz = (z + ring(s) + NZ) % NZ

        def chunk(h):
            ch = 2 * zz + h
            tk = tok_all[pl.ds(2 * ch, 2)].reshape(CHUNK, WIDTH)
            raw = lax.dot_general(
                cen_aug[...], jnp.concatenate([tk, ones], axis=1),
                (((1,), (1,)), ((), ())), preferred_element_type=jnp.float32,
            )
            top = jnp.max(raw, axis=0, keepdims=True)
            e = jnp.exp2((raw - top) * unit)
            e_ref[:, pl.ds(pl.multiple_of(ch * CHUNK, CHUNK), CHUNK)] = e.astype(jnp.bfloat16)
            total = jnp.sum(e, axis=0, keepdims=True)
            m_ref[pl.ds(ch, 1)] = (top * unit)[None]
            part = top * unit + jnp.log2(total)
            l_send[pl.ds(ch, 1)] = part[None]

            @pl.when(ch != n)
            def _():
                lc_copy(ch).start()

            @pl.when(ch == n)
            def _():
                l_cen[pl.ds(ch, 1)] = part[None]

        loop(0, 2, chunk)

    def py_copy(r):
        to = (y + r) % NY
        return copy(py.at[to], pr.at[r], py_s.at[r], py_r.at[r], (t, to * 2 + c))

    def pick():
        loop(1, N_TOK, lambda r: ids_copy(r).wait_recv())
        cen_copy().wait_recv()
        first = (t * N_CEN + y * 2) * LOCAL
        rel = (ids_all[...].reshape(N_TOK, ROWS) - first).astype(jnp.float32)
        rel = jnp.transpose(rel).reshape(NY, 2, 8, N_TOK)
        rel = jnp.where(c == 0, rel[:, 0], rel[:, 1]).reshape(NY * 8, N_TOK)
        for p in range(N_TOK // 2):
            one = jnp.broadcast_to(rel[:, 2 * p : 2 * p + 1], (NY * 8, WIDTH)).reshape(NY, 1, 8, WIDTH)
            two = jnp.broadcast_to(rel[:, 2 * p + 1 : 2 * p + 2], (NY * 8, WIDTH)).reshape(NY, 1, 8, WIDTH)
            cols[p] = jnp.concatenate([one, two], axis=1).reshape(ROWS, WIDTH)
        at = lax.broadcasted_iota(jnp.int32, (1, WIDTH), 1).astype(jnp.float32)

        def part(g):
            want = cols[pl.ds(4 * g, 4)].reshape(4 * ROWS, WIDTH)
            hot = jnp.concatenate(
                [jnp.where(want == at + float(WIDTH * b), 1.0, 0.0).astype(jnp.bfloat16) for b in range(2 * LOCAL // WIDTH)],
                axis=1,
            )
            got = jnp.dot(hot, cen2[...].reshape(2 * LOCAL, WIDTH), preferred_element_type=jnp.float32)
            got = got.astype(jnp.bfloat16).reshape(4, NY, 16, WIDTH)
            for k in range(4):
                py[:, pl.ds(pl.multiple_of((4 * g + k) * 16, 16), 16), :] = got[k]

        loop(0, 4, part)
        loop(1, NY, lambda r: py_copy(r).start())

    def step(s):
        @pl.when(s < NZ)
        def _():
            receive(s)

        @pl.when(s > 0)
        def _():
            score(s - 1)

        @pl.when(s == 4)
        def _():
            pick()

    loop(0, NZ + 1, step)

    def lse(v):
        top = jnp.max(v, axis=0)
        return top + jnp.log2(jnp.sum(jnp.exp2(v - top[None]), axis=0))

    def lc_wait(r):
        src = (n + r) % N_CEN
        copy(l_send.at[src], l_cen.at[src], lc_s.at[src], lc_r.at[src], (t, src)).wait_recv()

    def lt_copy(r):
        return copy(l_tok.at[t], l_tok.at[t], lt_s.at[r], lt_r.at[r], ((t + r) % N_TOK, n))

    def la_copy(r):
        return copy(l_all.at[n], l_all.at[n], la_s.at[r], la_r.at[r], (t, (n + r) % N_CEN))

    loop(1, N_CEN, lc_wait)
    l_tok[pl.ds(t, 1)] = lse(l_cen[...])[None]
    loop(1, N_TOK, lambda r: lt_copy(r).start())

    def rt_copy(r):
        to = (t + r) % N_TOK
        return copy(r_send.at[to], r_recv.at[t], rt_s.at[r], rt_r.at[r], (to, n))

    loop(1, NY, lambda r: py_copy(r).wait_recv())
    rows = py[pl.ds(y, 1)][0].astype(jnp.float32)
    for r in range(1, NY):
        rows = rows + pr[r].astype(jnp.float32)
    r_send[...] = rows.reshape(N_TOK, 8, WIDTH)
    loop(1, N_TOK, lambda r: rt_copy(r).start())
    r_recv[pl.ds(t, 1)] = r_send[pl.ds(t, 1)]

    loop(1, N_TOK, lambda r: lt_copy(r).wait_recv())
    l_all[pl.ds(n, 1)] = lse(l_tok[...])[None]
    loop(1, N_CEN, lambda r: la_copy(r).start())
    loop(1, N_CEN, lambda r: la_copy(r).wait_recv())

    for ch in range(N_CEN):
        g = jnp.exp2(m_ref[ch] - l_all[ch])
        flat[2 * ch : 2 * ch + 1, :] = g[:, :ROWS]
        flat[2 * ch + 1 : 2 * ch + 2, :] = g[:, ROWS:]
    g_cols = jnp.transpose(flat[...])
    for i in range(N_TOK):
        g = jnp.broadcast_to(g_cols[:, i : i + 1], (ROWS, WIDTH))
        g_hi = g.astype(jnp.bfloat16).astype(jnp.float32)
        g_ref[i * ROWS : (i + 1) * ROWS, :WIDTH] = (tok_all[i].astype(jnp.float32) * g).astype(jnp.bfloat16)
        g_ref[i * ROWS : (i + 1) * ROWS, WIDTH:] = jnp.where(lane < 64, g_hi, g - g_hi).astype(jnp.bfloat16)

    def final(j):
        at = pl.ds(pl.multiple_of(j * 256, 256), 256)
        out = jnp.dot(e_ref[at, :], g_ref[...], preferred_element_type=jnp.float32)
        mass = out[:, WIDTH : WIDTH + 1] + out[:, WIDTH + 64 : WIDTH + 65]
        upd_ref[at, :] = (out[:, :WIDTH] / mass).astype(jnp.bfloat16)

    loop(0, LOCAL // 256, final)

    own = l_all[pl.ds(t // 2, 1)][0] * LN2
    norm_ref[...] = jnp.where(t % 2 == 0, own[:, :ROWS], own[:, ROWS:])

    loop(1, N_TOK, lambda r: rt_copy(r).wait_recv())
    picked = jnp.sum(r_recv[...], axis=0)
    res_ref[...] = tok_f32[pl.ds(pl.multiple_of(n * 8, 8), 8), :] - picked

    def sent_tokens(s):
        for q in range(2):
            @pl.when(mine(s, q, c))
            def _():
                tok_copy(s, q).wait_send()
                fwd_copy(s, q).wait_send()

    loop(0, NZ, sent_tokens)
    cen_copy().wait_send()

    def sent_tok(r):
        ids_copy(r).wait_send()
        lt_copy(r).wait_send()
        rt_copy(r).wait_send()

    def sent_cen(r):
        lc_copy((n + r) % N_CEN).wait_send()
        la_copy(r).wait_send()

    loop(1, N_TOK, sent_tok)
    loop(1, N_CEN, sent_cen)
    loop(1, NY, lambda r: py_copy(r).wait_send())


def per_device(tokens, nearest, centroids, log_prior):
    bf, f32, dma = jnp.bfloat16, jnp.float32, pltpu.SemaphoreType.DMA
    upd, norm, res = pl.pallas_call(
        kernel,
        out_shape=(
            jax.ShapeDtypeStruct((LOCAL, WIDTH), bf),
            jax.ShapeDtypeStruct((1, ROWS), f32),
            jax.ShapeDtypeStruct((8, WIDTH), f32),
        ),
        in_specs=[pl.BlockSpec(memory_space=pltpu.VMEM)] * 4,
        out_specs=(pl.BlockSpec(memory_space=pltpu.VMEM),) * 3,
        scratch_shapes=[
            pltpu.VMEM((N_TOK, ROWS, WIDTH), bf),
            pltpu.VMEM((N_TOK, 1, ROWS), jnp.int32),
            pltpu.VMEM((2, LOCAL, WIDTH), bf),
            pltpu.VMEM((LOCAL, 2 * WIDTH), bf),
            pltpu.VMEM((LOCAL, N_TOK * ROWS), bf),
            pltpu.VMEM((N_TOK * ROWS, 2 * WIDTH), bf),
            pltpu.VMEM((N_CEN, 1, CHUNK), f32),
            pltpu.VMEM((N_CEN, 1, CHUNK), f32),
            pltpu.VMEM((N_CEN, 1, CHUNK), f32),
            pltpu.VMEM((N_TOK, 1, CHUNK), f32),
            pltpu.VMEM((N_CEN, 1, CHUNK), f32),
            pltpu.VMEM((N_TOK, ROWS), f32),
            pltpu.VMEM((N_TOK // 2, ROWS, WIDTH), f32),
            pltpu.VMEM((NY, N_TOK * 8, WIDTH), bf),
            pltpu.VMEM((NY, N_TOK * 8, WIDTH), bf),
            pltpu.VMEM((N_TOK, 8, WIDTH), f32),
            pltpu.VMEM((N_TOK, 8, WIDTH), f32),
            pltpu.VMEM((ROWS, WIDTH), f32),
            dma((NZ, 2)), dma((NZ, 2)), dma((NZ, 2)), dma((NZ, 2)),
            dma((N_TOK,)), dma((N_TOK,)), dma, dma,
            dma((N_CEN,)), dma((N_CEN,)), dma((N_TOK,)), dma((N_TOK,)),
            dma((N_CEN,)), dma((N_CEN,)), dma((NY,)), dma((NY,)),
            dma((N_TOK,)), dma((N_TOK,)),
        ],
        compiler_params=pltpu.CompilerParams(
            collective_id=0, has_side_effects=True, vmem_limit_bytes=48 << 20
        ),
    )(tokens, nearest.reshape(1, ROWS), centroids, log_prior.reshape(LOCAL // ROWS, ROWS))
    return upd, norm.reshape(ROWS), res.astype(bf)


def solution(mesh):
    return jax.shard_map(
        per_device,
        mesh=mesh,
        in_specs=(P("tok", None), P("tok"), P(("tok", "cen"), None), P(("tok", "cen"))),
        out_specs=(P(("tok", "cen"), None), P("tok"), P(("tok", "cen"), None)),
        check_vma=False,
    )
```

```python
import functools
import math

import jax
import jax.numpy as jnp
from jax import lax
from jax.experimental import pallas as pl
from jax.experimental.pallas import tpu as pltpu
from jax.sharding import PartitionSpec as P

MESH = pl.DeviceIdType.MESH
NX, NY, NZ = 4, 8, 8
N_TOK, N_CEN = 32, 16
ROWS = 128
WIDTH = 128
LOCAL = 1024
CHUNK = 256
LN2 = math.log(2.0)
VMEM_LIMIT = 60 << 20


def ring(s):
    half = (s + 1) // 2
    return half * (2 * (s % 2) - 1)


def loop(lo, hi, body):
    def step(i, carry):
        body(i)
        return carry

    lax.fori_loop(lo, hi, step, 0)


def split3(v):
    hi = v.astype(jnp.bfloat16).astype(jnp.float32)
    mid = (v - hi).astype(jnp.bfloat16).astype(jnp.float32)
    return hi, mid, v - hi - mid


def kernel(
    tok_hbm, ids_hbm, cen_hbm, lp_hbm, upd_ref, norm_ref, res_ref,
    tok_all, ids_all, cen2, lp_ref, cen_aug, e_ref, acc, m_ref, l_send, l_cen, l_tok, l_all,
    cols, ya_out, ya_in, ta_out, ta_in, xb_out, xb_in, yb_out, yb_in, zb_out, zb_in, tok_f32,
    in_s, z_s, z_r, x_s, x_r, f_s, f_r, idz_s, idz_r, idx_s, idx_r, cen_s, cen_r,
    lc_s, lc_r, lt_s, lt_r, la_s, la_r, ya_s, ya_r, ta_s, ta_r, xb_s, xb_r, yb_s, yb_r, zb_s, zb_r,
):
    t = lax.axis_index("tok")
    n = lax.axis_index("cen")
    x, z = t % NX, t // NX
    y, c = n // 2, n % 2
    sib = (t, y * 2 + 1 - c)
    unit = math.log2(math.e) / math.sqrt(WIDTH)

    def at_x(k):
        return (z * NX + (x + k) % NX, n)

    def at_y(k):
        return (t, ((y + k) % NY) * 2 + c)

    def at_z(k):
        return (((z + k) % NZ) * NX + x, n)

    def copy(src, dst, send, recv, dev):
        return pltpu.make_async_remote_copy(
            src_ref=src, dst_ref=dst, send_sem=send, recv_sem=recv, device_id=dev, device_id_type=MESH
        )

    barrier = pltpu.get_barrier_semaphore()

    def greet(dev):
        pl.semaphore_signal(barrier, inc=1, device_id=dev, device_id_type=MESH)

    loop(1, NZ, lambda k: greet(at_z(k)))
    loop(1, NY, lambda k: greet(at_y(k)))
    loop(1, NX, lambda k: greet(at_x(k)))
    greet(sib)

    fetch = [
        pltpu.make_async_copy(tok_hbm, tok_all.at[t], in_s.at[0]),
        pltpu.make_async_copy(ids_hbm, ids_all.at[x * NZ + z], in_s.at[1]),
        pltpu.make_async_copy(cen_hbm, cen2.at[c], in_s.at[2]),
        pltpu.make_async_copy(lp_hbm, lp_ref, in_s.at[3]),
    ]
    for f in fetch:
        f.start()
    for f in fetch:
        f.wait()
    tok_f32[...] = tok_all[pl.ds(t, 1)][0].astype(jnp.float32)
    lane = lax.broadcasted_iota(jnp.int32, (ROWS, WIDTH), 1)
    lp_cols = jnp.transpose(lp_ref[...] * math.sqrt(WIDTH))
    for a in range(LOCAL // ROWS):
        hi, mid, low = split3(lp_cols[:, a : a + 1])
        extra = jnp.where(lane == 0, hi, jnp.where(lane == 1, mid, jnp.where(lane == 2, low, 0.0)))
        cen_aug[a * ROWS : (a + 1) * ROWS, WIDTH:] = extra.astype(jnp.bfloat16)
    cen_aug[:, :WIDTH] = cen2[pl.ds(c, 1)][0]

    pl.semaphore_wait(barrier, NZ - 1 + NY - 1 + NX - 1 + 1)

    def idz_copy(k):
        return copy(ids_all.at[x * NZ + z], ids_all.at[x * NZ + z], idz_s.at[k], idz_r.at[k], at_z(k))

    def idx_copy(k):
        rows = pl.ds(x * NZ, NZ)
        return copy(ids_all.at[rows], ids_all.at[rows], idx_s.at[k], idx_r.at[k], at_x(k))

    def cen_copy():
        return copy(cen2.at[c], cen2.at[c], cen_s, cen_r, sib)

    def z_copy(s):
        return copy(tok_all.at[t], tok_all.at[t], z_s.at[s], z_r.at[s], at_z(NZ - ring(s)))

    def block(s, k):
        return ((z + ring(s) + NZ) % NZ) * NX + (x + k) % NX

    def x_copy(s, k):
        b = block(s, 0)
        return copy(tok_all.at[b], tok_all.at[b], x_s.at[s, k], x_r.at[s, k], at_x(NX - k))

    def f_copy(s, k):
        b = block(s, k)
        return copy(tok_all.at[b], tok_all.at[b], f_s.at[s, k], f_r.at[s, k], sib)

    def if_mine(s, core, todo):
        pl.when(s % 2 == core)(todo)

    loop(1, NZ, lambda k: idz_copy(k).start())
    loop(1, NZ, lambda s: if_mine(s, c, lambda: z_copy(s).start()))
    cen_copy().start()

    def receive_z(s):
        def todo():
            @pl.when(s > 0)
            def _():
                z_copy(s).wait_recv()

            for k in range(1, NX):
                x_copy(s, k).start()

            @pl.when(s > 0)
            def _():
                f_copy(s, 0).start()

        if_mine(s, c, todo)

    def receive_x(s):
        def todo():
            for k in range(1, NX):
                x_copy(s, k).wait_recv()
                f_copy(s, k).start()

        if_mine(s, c, todo)

    ones = jnp.where(lax.broadcasted_iota(jnp.int32, (CHUNK, WIDTH), 1) < 3, 1.0, 0.0).astype(jnp.bfloat16)

    def lc_copy(ch):
        return copy(l_send.at[ch], l_cen.at[n], lc_s.at[ch], lc_r.at[n], (t, ch))

    def score(s):
        def todo():
            @pl.when(s > 0)
            def _():
                f_copy(s, 0).wait_recv()

            for k in range(1, NX):
                f_copy(s, k).wait_recv()

        if_mine(s, 1 - c, todo)
        zz = (z + ring(s) + NZ) % NZ
        parts = []
        for h in range(2):
            ch = 2 * zz + h
            tk = tok_all[pl.ds(2 * ch, 2)].reshape(CHUNK, WIDTH)
            raw = lax.dot_general(
                cen_aug[...], jnp.concatenate([tk, ones], axis=1),
                (((1,), (1,)), ((), ())), preferred_element_type=jnp.float32,
            )
            top = jnp.max(raw, axis=0, keepdims=True)
            e = jnp.exp2((raw - top) * unit)
            e_ref[:, pl.ds(pl.multiple_of(ch * CHUNK, CHUNK), CHUNK)] = e.astype(jnp.bfloat16)
            total = jnp.sum(e, axis=0, keepdims=True)
            m_ref[pl.ds(ch, 1)] = (top * unit)[None]
            part = top * unit + jnp.log2(total)
            l_send[pl.ds(ch, 1)] = part[None]
            parts.append(part)
        for h in range(2):
            ch = 2 * zz + h
            part = parts[h]

            @pl.when(ch != n)
            def _():
                lc_copy(ch).start()

            @pl.when(ch == n)
            def _():
                l_cen[pl.ds(ch, 1)] = part[None]

    def ya_copy(k):
        return copy(ya_out.at[(y + k) % NY], ya_in.at[k], ya_s.at[k], ya_r.at[k], at_y(k))

    def xb_copy(k):
        return copy(xb_out.at[(x + k) % NX], xb_in.at[k], xb_s.at[k], xb_r.at[k], at_x(k))

    def yb_copy(k):
        return copy(yb_out.at[(y + k) % NY], yb_in.at[k], yb_s.at[k], yb_r.at[k], at_y(k))

    def pick():
        loop(1, NX, lambda k: idx_copy(k).wait_recv())
        first = (t * N_CEN + y * 2) * LOCAL
        rel = (ids_all[...].reshape(N_TOK, ROWS) - first).astype(jnp.float32)
        rel = jnp.transpose(rel).reshape(NY, 2, 8, N_TOK)
        rel = jnp.where(c == 0, rel[:, 0], rel[:, 1]).reshape(NY * 8, N_TOK)

        def spread(zb, xb):
            i = xb * NZ + zb
            return jnp.broadcast_to(rel[:, i : i + 1], (NY * 8, WIDTH)).reshape(NY, 1, 8, WIDTH)

        for p in range(N_TOK // 2):
            if p < 8:
                one, two = (p // 2, (2 * p) % NX), (p // 2, (2 * p) % NX + 1)
            else:
                one, two = (2 * (p // 4), p % NX), (2 * (p // 4) + 1, p % NX)
            cols[p] = jnp.concatenate([spread(*one), spread(*two)], axis=1).reshape(ROWS, WIDTH)
        at = lax.broadcasted_iota(jnp.int32, (1, WIDTH), 1).astype(jnp.float32)

        def part(g):
            want = cols[pl.ds(4 * g, 4)].reshape(4 * ROWS, WIDTH)
            hot = jnp.concatenate(
                [jnp.where(want == at + float(WIDTH * b), 1.0, 0.0).astype(jnp.bfloat16) for b in range(2 * LOCAL // WIDTH)],
                axis=1,
            )
            got = jnp.dot(hot, cen2[...].reshape(2 * LOCAL, WIDTH), preferred_element_type=jnp.float32)
            return got.astype(jnp.bfloat16).reshape(4, NY, 16, WIDTH)

        def part_a(g):
            got = part(g)
            for k in range(4):
                ya_out[:, pl.ds(pl.multiple_of((4 * g + k) * 16, 16), 16), :] = got[k]

        def part_b(g):
            got = part(g)
            for k in range(4):
                xb_out[k, :, pl.ds(pl.multiple_of((g - 2) * 16, 16), 16), :] = got[k]

        loop(0, 2, part_a)
        loop(1, NY, lambda k: ya_copy(k).start())
        loop(2, 4, part_b)
        loop(1, NX, lambda k: xb_copy(k).start())

    def ids_along_x():
        loop(1, NZ, lambda k: idz_copy(k).wait_recv())
        loop(1, NX, lambda k: idx_copy(k).start())

    receive_z(0)
    cen_copy().wait_recv()
    loop(1, 3, receive_z)
    receive_x(0)
    loop(3, 5, receive_z)
    ids_along_x()

    def step(s):
        @pl.when(s == 1)
        def _():
            loop(5, NZ, receive_z)
            loop(1, 3, receive_x)

        @pl.when((s >= 1) & (s + 2 < NZ))
        def _():
            receive_x(s + 2)

        score(s)

    loop(0, NZ, step)
    pick()

    def tok_of(j):
        return ((z + ring(7 - j // NX) + NZ) % NZ) * NX + (x + 1 + j % NX) % NX

    def cen_of(j):
        return ((y + ring(7 - j // 2) + NY) % NY) * 2 + (c + 1 + j) % 2

    def lse(v):
        top = jnp.max(v, axis=0)
        return top + jnp.log2(jnp.sum(jnp.exp2(v - top[None]), axis=0))

    def lc_wait(j):
        src = cen_of(j)
        copy(l_send.at[src], l_cen.at[src], lc_s.at[src], lc_r.at[src], (t, src)).wait_recv()

    def lt_copy(to):
        return copy(l_tok.at[t], l_tok.at[t], lt_s.at[to], lt_r.at[t], (to, n))

    def lt_wait(j):
        src = tok_of(j)
        copy(l_tok.at[src], l_tok.at[src], lt_s.at[src], lt_r.at[src], (src, n)).wait_recv()

    def la_copy(to):
        return copy(l_all.at[n], l_all.at[n], la_s.at[to], la_r.at[n], (t, to))

    def la_wait(src):
        copy(l_all.at[src], l_all.at[src], la_s.at[src], la_r.at[src], (t, src)).wait_recv()

    def ta_copy(to):
        return copy(ta_out.at[to], ta_in.at[t], ta_s.at[to], ta_r.at[t], (to, n))

    def ta_wait(src):
        copy(ta_out.at[0], ta_in.at[src], ta_s.at[0], ta_r.at[src], (src, n)).wait_recv()

    half = NZ // 2

    def zb_copy(zt):
        dev = (zt * NX + x, n)
        return copy(zb_out.at[zt - half], zb_in.at[z], zb_s.at[zt], zb_r.at[z], dev)

    def zb_wait(src):
        copy(zb_out.at[0], zb_in.at[src], zb_s.at[0], zb_r.at[src], (src * NX + x, n)).wait_recv()

    loop(1, NX, lambda k: xb_copy(k).wait_recv())
    rows = xb_out[pl.ds(x, 1)][0].astype(jnp.float32)
    for k in range(1, NX):
        rows = rows + xb_in[k].astype(jnp.float32)
    yb_out[...] = rows.astype(jnp.bfloat16)
    loop(1, NY, lambda k: yb_copy(k).start())

    loop(0, N_CEN - 1, lc_wait)
    l_tok[pl.ds(t, 1)] = lse(l_cen[...])[None]
    loop(0, N_TOK - 1, lambda j: lt_copy(tok_of(j)).start())

    loop(1, NY, lambda k: ya_copy(k).wait_recv())
    rows = ya_out[pl.ds(y, 1)][0].astype(jnp.float32)
    for k in range(1, NY):
        rows = rows + ya_in[k].astype(jnp.float32)
    ta_out[...] = rows.reshape(half * NX, 8, WIDTH)

    def ta_each(act):
        def body(to):
            @pl.when(to != t)
            def _():
                act(to)

        loop(0, half * NX, body)

    ta_each(lambda to: ta_copy(to).start())

    loop(1, NY, lambda k: yb_copy(k).wait_recv())
    rows = yb_out[pl.ds(y, 1)][0].astype(jnp.float32)
    for k in range(1, NY):
        rows = rows + yb_in[k].astype(jnp.float32)
    zb_out[...] = rows.reshape(half, 8, WIDTH)

    def zb_each(act):
        def body(zt):
            @pl.when(zt != z)
            def _():
                act(zt)

        loop(half, NZ, body)

    zb_each(lambda zt: zb_copy(zt).start())

    loop(0, N_TOK - 1, lt_wait)
    l_all[pl.ds(n, 1)] = lse(l_tok[...])[None]
    loop(0, N_CEN - 1, lambda j: la_copy(cen_of(j)).start())

    def product(k):
        yy = (y + ring(k) + NY) % NY
        rows = []
        for h in range(2):
            ch = 2 * yy + h
            g_row = jnp.exp2(m_ref[pl.ds(ch, 1)][0] - l_all[pl.ds(ch, 1)][0])
            for b in range(2):
                g = jnp.transpose(jnp.broadcast_to(g_row[:, b * ROWS : (b + 1) * ROWS], (WIDTH, ROWS)))
                g_hi = g.astype(jnp.bfloat16).astype(jnp.float32)
                tk = tok_all[pl.ds(2 * ch + b, 1)][0].astype(jnp.float32)
                rows.append(
                    jnp.concatenate([tk * g, jnp.where(lane < 64, g_hi, g - g_hi)], axis=1).astype(jnp.bfloat16)
                )
        e = e_ref[:, pl.ds(pl.multiple_of(yy * 2 * CHUNK, 2 * CHUNK), 2 * CHUNK)]
        return jnp.dot(e, jnp.concatenate(rows, axis=0), preferred_element_type=jnp.float32)

    for group in ((0,), (1, 2), (3, 4), (5, 6, 7)):
        for k in group:
            for h in range(2):
                ch = 2 * ((y + ring(k) + NY) % NY) + h

                @pl.when(ch != n)
                def _():
                    la_wait(ch)

        for k in group:
            if k == 0:
                acc[...] = product(k)
            else:
                acc[...] += product(k)
    mass = acc[:, WIDTH:]
    mass = mass + pltpu.roll(mass, 64, 1)
    upd_ref[...] = (acc[:, :WIDTH] / mass).astype(jnp.bfloat16)

    own = l_all[pl.ds(t // 2, 1)][0] * LN2
    norm_ref[...] = jnp.where(t % 2 == 0, own[:, :ROWS], own[:, ROWS:])

    mine = tok_f32[pl.ds(pl.multiple_of(n * 8, 8), 8), :]

    @pl.when(z < half)
    def _():
        ta_in[pl.ds(t, 1)] = ta_out[pl.ds(t, 1)]
        loop(0, N_TOK - 1, lambda j: ta_wait(tok_of(j)))
        res_ref[...] = (mine - jnp.sum(ta_in[...], axis=0)).astype(jnp.bfloat16)

    @pl.when(z >= half)
    def _():
        zb_in[pl.ds(z, 1)] = zb_out[pl.ds(z - half, 1)]
        loop(1, NZ, lambda k: zb_wait((z + k) % NZ))
        res_ref[...] = (mine - jnp.sum(zb_in[...], axis=0)).astype(jnp.bfloat16)

    def sent(s):
        def todo():
            @pl.when(s > 0)
            def _():
                z_copy(s).wait_send()
                f_copy(s, 0).wait_send()

            for k in range(1, NX):
                x_copy(s, k).wait_send()
                f_copy(s, k).wait_send()

        if_mine(s, c, todo)

    loop(0, NZ, sent)
    cen_copy().wait_send()

    def sent_axis(k):
        idz_copy(k).wait_send()
        ya_copy(k).wait_send()
        yb_copy(k).wait_send()

    def sent_x(k):
        idx_copy(k).wait_send()
        xb_copy(k).wait_send()

    def sent_cen(j):
        lc_copy(cen_of(j)).wait_send()
        la_copy(cen_of(j)).wait_send()

    loop(1, NZ, sent_axis)
    loop(1, NX, sent_x)
    loop(0, N_CEN - 1, sent_cen)
    loop(0, N_TOK - 1, lambda j: lt_copy(tok_of(j)).wait_send())
    ta_each(lambda to: ta_copy(to).wait_send())
    zb_each(lambda zt: zb_copy(zt).wait_send())


def hand_on(upd_in, norm_in, res_in, upd_ref, norm_ref, res_ref):
    upd_ref[...] = upd_in[...]
    norm_ref[...] = norm_in[...]
    res_ref[...] = res_in[...]


def per_device(tokens, nearest, centroids, log_prior):
    bf, f32, dma, vmem = jnp.bfloat16, jnp.float32, pltpu.SemaphoreType.DMA, pltpu.VMEM
    upd, norm, res = pl.pallas_call(
        kernel,
        out_shape=(
            jax.ShapeDtypeStruct((LOCAL, WIDTH), bf),
            jax.ShapeDtypeStruct((1, ROWS), f32),
            jax.ShapeDtypeStruct((8, WIDTH), bf),
        ),
        in_specs=[pl.BlockSpec(memory_space=pltpu.HBM)] * 4,
        out_specs=(pl.BlockSpec(memory_space=pltpu.VMEM),) * 3,
        scratch_shapes=[
            vmem((N_TOK, ROWS, WIDTH), bf),
            vmem((N_TOK, 1, ROWS), jnp.int32),
            vmem((2, LOCAL, WIDTH), bf),
            vmem((LOCAL // ROWS, ROWS), f32),
            vmem((LOCAL, 2 * WIDTH), bf),
            vmem((LOCAL, N_TOK * ROWS), bf),
            vmem((LOCAL, 2 * WIDTH), f32),
            vmem((N_CEN, 1, CHUNK), f32),
            vmem((N_CEN, 1, CHUNK), f32),
            vmem((N_CEN, 1, CHUNK), f32),
            vmem((N_TOK, 1, CHUNK), f32),
            vmem((N_CEN, 1, CHUNK), f32),
            vmem((N_TOK // 2, ROWS, WIDTH), f32),
            vmem((NY, ROWS, WIDTH), bf), vmem((NY, ROWS, WIDTH), bf),
            vmem((N_TOK // 2, 8, WIDTH), f32), vmem((N_TOK, 8, WIDTH), f32),
            vmem((NX, NY, 32, WIDTH), bf), vmem((NX, NY, 32, WIDTH), bf),
            vmem((NY, 32, WIDTH), bf), vmem((NY, 32, WIDTH), bf),
            vmem((NZ // 2, 8, WIDTH), f32), vmem((NZ, 8, WIDTH), f32),
            vmem((ROWS, WIDTH), f32),
            dma((4,)), dma((NZ,)), dma((NZ,)), dma((NZ, NX)), dma((NZ, NX)), dma((NZ, NX)), dma((NZ, NX)),
            dma((NZ,)), dma((NZ,)), dma((NX,)), dma((NX,)), dma, dma,
            dma((N_CEN,)), dma((N_CEN,)), dma((N_TOK,)), dma((N_TOK,)), dma((N_CEN,)), dma((N_CEN,)),
            dma((NY,)), dma((NY,)), dma((N_TOK,)), dma((N_TOK,)), dma((NX,)), dma((NX,)),
            dma((NY,)), dma((NY,)), dma((NZ,)), dma((NZ,)),
        ],
        compiler_params=pltpu.CompilerParams(
            collective_id=0, has_side_effects=True, vmem_limit_bytes=VMEM_LIMIT
        ),
    )(tokens, nearest.reshape(1, ROWS), centroids, log_prior.reshape(LOCAL // ROWS, ROWS))
    upd, norm, res = pl.pallas_call(
        hand_on,
        out_shape=tuple(jax.ShapeDtypeStruct(v.shape, v.dtype) for v in (upd, norm, res)),
        in_specs=[pl.BlockSpec(memory_space=pltpu.VMEM)] * 3,
        out_specs=(pl.BlockSpec(memory_space=pltpu.VMEM),) * 3,
        compiler_params=pltpu.CompilerParams(vmem_limit_bytes=VMEM_LIMIT),
    )(upd, norm, res)
    return upd, norm.reshape(ROWS), res


def solution(mesh):
    return jax.shard_map(
        per_device,
        mesh=mesh,
        in_specs=(P("tok", None), P("tok"), P(("tok", "cen"), None), P(("tok", "cen"))),
        out_specs=(P(("tok", "cen"), None), P("tok"), P(("tok", "cen"), None)),
        check_vma=False,
    )
```

```python
import functools
import math

import jax
import jax.numpy as jnp
from jax import lax
from jax.experimental import pallas as pl
from jax.experimental.pallas import tpu as pltpu
from jax.sharding import PartitionSpec as P

MESH = pl.DeviceIdType.MESH
NX, NY, NZ = 4, 8, 8
N_TOK, N_CEN = 32, 16
ROWS = 128
WIDTH = 128
LOCAL = 1024
CHUNK = 256
LN2 = math.log(2.0)
VMEM_LIMIT = 60 << 20
PICK_B, PICK_A = 8, 8


def ring(s):
    half = (s + 1) // 2
    return half * (2 * (s % 2) - 1)


def loop(lo, hi, body):
    def step(i, carry):
        body(i)
        return carry

    lax.fori_loop(lo, hi, step, 0)


def split3(v):
    hi = v.astype(jnp.bfloat16).astype(jnp.float32)
    mid = (v - hi).astype(jnp.bfloat16).astype(jnp.float32)
    return hi, mid, v - hi - mid


def kernel(
    tok_hbm, ids_hbm, cen_hbm, lp_hbm, upd_ref, norm_ref, res_ref,
    tok_all, ids_all, cen2, lp_ref, cen_aug, tok_t, e_ref, acc, m_ref, l_send, l_cen, l_tok, l_all,
    cols, ya_out, ya_in, ta_out, ta_in, xb_out, xb_in, yb_out, yb_in, zb_out, zb_in, tok_f32,
    in_s, z_s, z_r, x_s, x_r, f_s, f_r, idz_s, idz_r, idx_s, idx_r, cen_s, cen_r,
    lc_s, lc_r, lt_s, lt_r, la_s, la_r, ya_s, ya_r, ta_s, ta_r, xb_s, xb_r, yb_s, yb_r, zb_s, zb_r,
):
    t = lax.axis_index("tok")
    n = lax.axis_index("cen")
    x, z = t % NX, t // NX
    y, c = n // 2, n % 2
    sib = (t, y * 2 + 1 - c)
    unit = math.log2(math.e) / math.sqrt(WIDTH)

    def at_x(k):
        return (z * NX + (x + k) % NX, n)

    def at_y(k):
        return (t, ((y + k) % NY) * 2 + c)

    def at_z(k):
        return (((z + k) % NZ) * NX + x, n)

    def copy(src, dst, send, recv, dev):
        return pltpu.make_async_remote_copy(
            src_ref=src, dst_ref=dst, send_sem=send, recv_sem=recv, device_id=dev, device_id_type=MESH
        )

    barrier = pltpu.get_barrier_semaphore()

    def greet(dev):
        pl.semaphore_signal(barrier, inc=1, device_id=dev, device_id_type=MESH)

    loop(1, NZ, lambda k: greet(at_z(k)))
    loop(1, NY, lambda k: greet(at_y(k)))
    loop(1, NX, lambda k: greet(at_x(k)))
    greet(sib)

    fetch = [
        pltpu.make_async_copy(tok_hbm, tok_all.at[t], in_s.at[0]),
        pltpu.make_async_copy(ids_hbm, ids_all.at[x * NZ + z], in_s.at[1]),
        pltpu.make_async_copy(cen_hbm, cen2.at[c], in_s.at[2]),
        pltpu.make_async_copy(lp_hbm, lp_ref, in_s.at[3]),
    ]
    for f in fetch:
        f.start()
    for f in fetch:
        f.wait()
    tok_f32[...] = tok_all[pl.ds(t, 1)][0].astype(jnp.float32)
    lane = lax.broadcasted_iota(jnp.int32, (ROWS, WIDTH), 1)
    lp_cols = jnp.transpose(lp_ref[...] * math.sqrt(WIDTH))
    for a in range(LOCAL // ROWS):
        hi, mid, low = split3(lp_cols[:, a : a + 1])
        extra = jnp.where(lane == 0, hi, jnp.where(lane == 1, mid, jnp.where(lane == 2, low, 0.0)))
        cen_aug[a * ROWS : (a + 1) * ROWS, WIDTH:] = extra.astype(jnp.bfloat16)
    cen_aug[:LOCAL, :WIDTH] = cen2[pl.ds(c, 1)][0]
    eye = lane == lax.broadcasted_iota(jnp.int32, (ROWS, WIDTH), 0)
    cen_aug[LOCAL:, :WIDTH] = jnp.where(eye, 1.0, 0.0).astype(jnp.bfloat16)
    cen_aug[LOCAL:, WIDTH:] = jnp.zeros((WIDTH, WIDTH), jnp.bfloat16)

    pl.semaphore_wait(barrier, NZ - 1 + NY - 1 + NX - 1 + 1)

    def idz_copy(k):
        return copy(ids_all.at[x * NZ + z], ids_all.at[x * NZ + z], idz_s.at[k], idz_r.at[k], at_z(k))

    def idx_copy(k):
        rows = pl.ds(x * NZ, NZ)
        return copy(ids_all.at[rows], ids_all.at[rows], idx_s.at[k], idx_r.at[k], at_x(k))

    def cen_copy():
        return copy(cen2.at[c], cen2.at[c], cen_s, cen_r, sib)

    def z_copy(s):
        return copy(tok_all.at[t], tok_all.at[t], z_s.at[s], z_r.at[s], at_z(NZ - ring(s)))

    def block(s, k):
        return ((z + ring(s) + NZ) % NZ) * NX + (x + k) % NX

    def x_copy(s, k):
        b = block(s, 0)
        return copy(tok_all.at[b], tok_all.at[b], x_s.at[s, k], x_r.at[s, k], at_x(NX - k))

    def f_copy(s, k):
        b = block(s, k)
        return copy(tok_all.at[b], tok_all.at[b], f_s.at[s, k], f_r.at[s, k], sib)

    def if_mine(s, core, todo):
        pl.when(s % 2 == core)(todo)

    loop(1, NZ, lambda k: idz_copy(k).start())
    loop(1, NZ, lambda s: if_mine(s, c, lambda: z_copy(s).start()))
    cen_copy().start()

    def receive_z(s):
        def todo():
            @pl.when(s > 0)
            def _():
                z_copy(s).wait_recv()

            for k in range(1, NX):
                x_copy(s, k).start()

            @pl.when(s > 0)
            def _():
                f_copy(s, 0).start()

        if_mine(s, c, todo)

    def receive_x(s):
        def todo():
            for k in range(1, NX):
                x_copy(s, k).wait_recv()
                f_copy(s, k).start()

        if_mine(s, c, todo)

    ones = jnp.where(lax.broadcasted_iota(jnp.int32, (CHUNK, WIDTH), 1) < 3, 1.0, 0.0).astype(jnp.bfloat16)

    def lc_copy(ch):
        return copy(l_send.at[ch], l_cen.at[n], lc_s.at[ch], lc_r.at[n], (t, ch))

    def score(s):
        def todo():
            @pl.when(s > 0)
            def _():
                f_copy(s, 0).wait_recv()

            for k in range(1, NX):
                f_copy(s, k).wait_recv()

        if_mine(s, 1 - c, todo)
        zz = (z + ring(s) + NZ) % NZ
        parts = []
        for h in range(2):
            ch = 2 * zz + h
            tk = tok_all[pl.ds(2 * ch, 2)].reshape(CHUNK, WIDTH)
            raw = lax.dot_general(
                cen_aug[...], jnp.concatenate([tk, ones], axis=1),
                (((1,), (1,)), ((), ())), preferred_element_type=jnp.float32,
            )
            tok_t[pl.ds(ch, 1)] = raw[LOCAL:].astype(jnp.bfloat16)[None]
            raw = raw[:LOCAL]
            top = jnp.max(raw, axis=0, keepdims=True)
            e = jnp.exp2((raw - top) * unit)
            e_ref[:, pl.ds(pl.multiple_of(ch * CHUNK, CHUNK), CHUNK)] = e.astype(jnp.bfloat16)
            total = jnp.sum(e, axis=0, keepdims=True)
            m_ref[pl.ds(ch, 1)] = (top * unit)[None]
            part = top * unit + jnp.log2(total)
            l_send[pl.ds(ch, 1)] = part[None]
            parts.append(part)
        for h in range(2):
            ch = 2 * zz + h
            part = parts[h]

            @pl.when(ch != n)
            def _():
                lc_copy(ch).start()

            @pl.when(ch == n)
            def _():
                l_cen[pl.ds(ch, 1)] = part[None]

    def ya_copy(k):
        return copy(ya_out.at[(y + k) % NY], ya_in.at[k], ya_s.at[k], ya_r.at[k], at_y(k))

    def xb_copy(k):
        return copy(xb_out.at[(x + k) % NX], xb_in.at[k], xb_s.at[k], xb_r.at[k], at_x(k))

    def yb_copy(k):
        return copy(yb_out.at[(y + k) % NY], yb_in.at[k], yb_s.at[k], yb_r.at[k], at_y(k))

    def pick_prepare():
        loop(1, NX, lambda k: idx_copy(k).wait_recv())
        first = (t * N_CEN + y * 2) * LOCAL
        rel = (ids_all[...].reshape(N_TOK, ROWS) - first).astype(jnp.float32)
        rel = jnp.transpose(rel).reshape(NY, 2, 8, N_TOK)
        rel = jnp.where(c == 0, rel[:, 0], rel[:, 1]).reshape(NY * 8, N_TOK)

        def spread(zb, xb):
            i = xb * NZ + zb
            return jnp.broadcast_to(rel[:, i : i + 1], (NY * 8, WIDTH)).reshape(NY, 1, 8, WIDTH)

        for p in range(N_TOK // 2):
            if p < 8:
                one, two = (p // 2, (2 * p) % NX), (p // 2, (2 * p) % NX + 1)
            else:
                one, two = (2 * (p // 4), p % NX), (2 * (p // 4) + 1, p % NX)
            cols[p] = jnp.concatenate([spread(*one), spread(*two)], axis=1).reshape(ROWS, WIDTH)

    def part(g):
        at = lax.broadcasted_iota(jnp.int32, (1, WIDTH), 1).astype(jnp.float32)
        want = cols[pl.ds(4 * g, 4)].reshape(4 * ROWS, WIDTH)
        hot = jnp.concatenate(
            [jnp.where(want == at + float(WIDTH * b), 1.0, 0.0).astype(jnp.bfloat16) for b in range(2 * LOCAL // WIDTH)],
            axis=1,
        )
        got = jnp.dot(hot, cen2[...].reshape(2 * LOCAL, WIDTH), preferred_element_type=jnp.float32)
        return got.astype(jnp.bfloat16).reshape(4, NY, 16, WIDTH)

    def part_a(g):
        got = part(g)
        for k in range(4):
            ya_out[:, pl.ds(pl.multiple_of((4 * g + k) * 16, 16), 16), :] = got[k]

    def part_b(g):
        got = part(g)
        for k in range(4):
            xb_out[k, :, pl.ds(pl.multiple_of((g - 2) * 16, 16), 16), :] = got[k]

    def pick_a():
        loop(0, 2, part_a)
        loop(1, NY, lambda k: ya_copy(k).start())

    def pick_b():
        pick_prepare()
        loop(2, 4, part_b)
        loop(1, NX, lambda k: xb_copy(k).start())

    def ids_along_x():
        loop(1, NZ, lambda k: idz_copy(k).wait_recv())
        loop(1, NX, lambda k: idx_copy(k).start())

    receive_z(0)
    cen_copy().wait_recv()
    loop(1, 3, receive_z)
    receive_x(0)
    loop(3, 5, receive_z)
    ids_along_x()

    def step(s):
        @pl.when(s == 1)
        def _():
            loop(5, NZ, receive_z)
            loop(1, 3, receive_x)

        @pl.when((s >= 1) & (s + 2 < NZ))
        def _():
            receive_x(s + 2)

        if PICK_B < NZ:
            pl.when(s == PICK_B)(pick_b)
        if PICK_A < NZ:
            pl.when(s == PICK_A)(pick_a)
        score(s)

    loop(0, NZ, step)
    if PICK_B >= NZ:
        pick_b()
    if PICK_A >= NZ:
        pick_a()

    def tok_of(j):
        return ((z + ring(7 - j // NX) + NZ) % NZ) * NX + (x + 1 + j % NX) % NX

    def cen_of(j):
        return ((y + ring(7 - j // 2) + NY) % NY) * 2 + (c + 1 + j) % 2

    def lse(v):
        top = jnp.max(v, axis=0)
        return top + jnp.log2(jnp.sum(jnp.exp2(v - top[None]), axis=0))

    def lc_wait(j):
        src = cen_of(j)
        copy(l_send.at[src], l_cen.at[src], lc_s.at[src], lc_r.at[src], (t, src)).wait_recv()

    def lt_copy(to):
        return copy(l_tok.at[t], l_tok.at[t], lt_s.at[to], lt_r.at[t], (to, n))

    def lt_wait(j):
        src = tok_of(j)
        copy(l_tok.at[src], l_tok.at[src], lt_s.at[src], lt_r.at[src], (src, n)).wait_recv()

    def la_copy(to):
        return copy(l_all.at[n], l_all.at[n], la_s.at[to], la_r.at[n], (t, to))

    def la_wait(src):
        copy(l_all.at[src], l_all.at[src], la_s.at[src], la_r.at[src], (t, src)).wait_recv()

    def ta_copy(to):
        return copy(ta_out.at[to], ta_in.at[t], ta_s.at[to], ta_r.at[t], (to, n))

    def ta_wait(src):
        copy(ta_out.at[0], ta_in.at[src], ta_s.at[0], ta_r.at[src], (src, n)).wait_recv()

    half = NZ // 2

    def zb_copy(zt):
        dev = (zt * NX + x, n)
        return copy(zb_out.at[zt - half], zb_in.at[z], zb_s.at[zt], zb_r.at[z], dev)

    def zb_wait(src):
        copy(zb_out.at[0], zb_in.at[src], zb_s.at[0], zb_r.at[src], (src * NX + x, n)).wait_recv()

    loop(0, N_CEN - 1, lc_wait)
    l_tok[pl.ds(t, 1)] = lse(l_cen[...])[None]
    loop(0, N_TOK - 1, lambda j: lt_copy(tok_of(j)).start())

    loop(1, NX, lambda k: xb_copy(k).wait_recv())
    rows = xb_out[pl.ds(x, 1)][0].astype(jnp.float32)
    for k in range(1, NX):
        rows = rows + xb_in[k].astype(jnp.float32)
    yb_out[...] = rows.astype(jnp.bfloat16)
    loop(1, NY, lambda k: yb_copy(k).start())

    loop(0, N_TOK - 1, lt_wait)
    l_all[pl.ds(n, 1)] = lse(l_tok[...])[None]
    loop(0, N_CEN - 1, lambda j: la_copy(cen_of(j)).start())

    loop(1, NY, lambda k: ya_copy(k).wait_recv())
    rows = ya_out[pl.ds(y, 1)][0].astype(jnp.float32)
    for k in range(1, NY):
        rows = rows + ya_in[k].astype(jnp.float32)
    ta_out[...] = rows.reshape(half * NX, 8, WIDTH)

    def ta_each(act):
        def body(to):
            @pl.when(to != t)
            def _():
                act(to)

        loop(0, half * NX, body)

    ta_each(lambda to: ta_copy(to).start())

    loop(1, NY, lambda k: yb_copy(k).wait_recv())
    rows = yb_out[pl.ds(y, 1)][0].astype(jnp.float32)
    for k in range(1, NY):
        rows = rows + yb_in[k].astype(jnp.float32)
    zb_out[...] = rows.reshape(half, 8, WIDTH)

    def zb_each(act):
        def body(zt):
            @pl.when(zt != z)
            def _():
                act(zt)

        loop(half, NZ, body)

    zb_each(lambda zt: zb_copy(zt).start())

    upper = lax.broadcasted_iota(jnp.int32, (WIDTH, CHUNK), 0) < 64

    def product(k):
        yy = (y + ring(k) + NY) % NY
        total = None
        for h in range(2):
            ch = 2 * yy + h
            g = jnp.exp2(m_ref[pl.ds(ch, 1)][0] - l_all[pl.ds(ch, 1)][0])
            g_hi = g.astype(jnp.bfloat16).astype(jnp.float32)
            top = tok_t[pl.ds(ch, 1)][0].astype(jnp.float32) * g
            low = jnp.where(upper, g_hi, g - g_hi)
            e = e_ref[:, pl.ds(pl.multiple_of(ch * CHUNK, CHUNK), CHUNK)]
            out = lax.dot_general(
                e, jnp.concatenate([top, low], axis=0).astype(jnp.bfloat16),
                (((1,), (1,)), ((), ())), preferred_element_type=jnp.float32,
            )
            total = out if total is None else total + out
        return total

    for group in ((0,), (1, 2), (3, 4), (5, 6, 7)):
        for k in group:
            for h in range(2):
                ch = 2 * ((y + ring(k) + NY) % NY) + h

                @pl.when(ch != n)
                def _():
                    la_wait(ch)

        for k in group:
            if k == 0:
                acc[...] = product(k)
            else:
                acc[...] += product(k)
    mass = acc[:, WIDTH:]
    mass = mass + pltpu.roll(mass, 64, 1)
    upd_ref[...] = (acc[:, :WIDTH] / mass).astype(jnp.bfloat16)

    own = l_all[pl.ds(t // 2, 1)][0] * LN2
    norm_ref[...] = jnp.where(t % 2 == 0, own[:, :ROWS], own[:, ROWS:])

    mine = tok_f32[pl.ds(pl.multiple_of(n * 8, 8), 8), :]

    @pl.when(z < half)
    def _():
        ta_in[pl.ds(t, 1)] = ta_out[pl.ds(t, 1)]
        loop(0, N_TOK - 1, lambda j: ta_wait(tok_of(j)))
        res_ref[...] = (mine - jnp.sum(ta_in[...], axis=0)).astype(jnp.bfloat16)

    @pl.when(z >= half)
    def _():
        zb_in[pl.ds(z, 1)] = zb_out[pl.ds(z - half, 1)]
        loop(1, NZ, lambda k: zb_wait((z + k) % NZ))
        res_ref[...] = (mine - jnp.sum(zb_in[...], axis=0)).astype(jnp.bfloat16)

    def sent(s):
        def todo():
            @pl.when(s > 0)
            def _():
                z_copy(s).wait_send()
                f_copy(s, 0).wait_send()

            for k in range(1, NX):
                x_copy(s, k).wait_send()
                f_copy(s, k).wait_send()

        if_mine(s, c, todo)

    loop(0, NZ, sent)
    cen_copy().wait_send()

    def sent_axis(k):
        idz_copy(k).wait_send()
        ya_copy(k).wait_send()
        yb_copy(k).wait_send()

    def sent_x(k):
        idx_copy(k).wait_send()
        xb_copy(k).wait_send()

    def sent_cen(j):
        lc_copy(cen_of(j)).wait_send()
        la_copy(cen_of(j)).wait_send()

    loop(1, NZ, sent_axis)
    loop(1, NX, sent_x)
    loop(0, N_CEN - 1, sent_cen)
    loop(0, N_TOK - 1, lambda j: lt_copy(tok_of(j)).wait_send())
    ta_each(lambda to: ta_copy(to).wait_send())
    zb_each(lambda zt: zb_copy(zt).wait_send())


def hand_on(upd_in, norm_in, res_in, upd_ref, norm_ref, res_ref):
    upd_ref[...] = upd_in[...]
    norm_ref[...] = norm_in[...]
    res_ref[...] = res_in[...]


def per_device(tokens, nearest, centroids, log_prior):
    bf, f32, dma, vmem = jnp.bfloat16, jnp.float32, pltpu.SemaphoreType.DMA, pltpu.VMEM
    upd, norm, res = pl.pallas_call(
        kernel,
        out_shape=(
            jax.ShapeDtypeStruct((LOCAL, WIDTH), bf),
            jax.ShapeDtypeStruct((1, ROWS), f32),
            jax.ShapeDtypeStruct((8, WIDTH), bf),
        ),
        in_specs=[pl.BlockSpec(memory_space=pltpu.HBM)] * 4,
        out_specs=(pl.BlockSpec(memory_space=pltpu.VMEM),) * 3,
        scratch_shapes=[
            vmem((N_TOK, ROWS, WIDTH), bf),
            vmem((N_TOK, 1, ROWS), jnp.int32),
            vmem((2, LOCAL, WIDTH), bf),
            vmem((LOCAL // ROWS, ROWS), f32),
            vmem((LOCAL + WIDTH, 2 * WIDTH), bf),
            vmem((N_CEN, WIDTH, CHUNK), bf),
            vmem((LOCAL, N_TOK * ROWS), bf),
            vmem((LOCAL, 2 * WIDTH), f32),
            vmem((N_CEN, 1, CHUNK), f32),
            vmem((N_CEN, 1, CHUNK), f32),
            vmem((N_CEN, 1, CHUNK), f32),
            vmem((N_TOK, 1, CHUNK), f32),
            vmem((N_CEN, 1, CHUNK), f32),
            vmem((N_TOK // 2, ROWS, WIDTH), f32),
            vmem((NY, ROWS, WIDTH), bf), vmem((NY, ROWS, WIDTH), bf),
            vmem((N_TOK // 2, 8, WIDTH), f32), vmem((N_TOK, 8, WIDTH), f32),
            vmem((NX, NY, 32, WIDTH), bf), vmem((NX, NY, 32, WIDTH), bf),
            vmem((NY, 32, WIDTH), bf), vmem((NY, 32, WIDTH), bf),
            vmem((NZ // 2, 8, WIDTH), f32), vmem((NZ, 8, WIDTH), f32),
            vmem((ROWS, WIDTH), f32),
            dma((4,)), dma((NZ,)), dma((NZ,)), dma((NZ, NX)), dma((NZ, NX)), dma((NZ, NX)), dma((NZ, NX)),
            dma((NZ,)), dma((NZ,)), dma((NX,)), dma((NX,)), dma, dma,
            dma((N_CEN,)), dma((N_CEN,)), dma((N_TOK,)), dma((N_TOK,)), dma((N_CEN,)), dma((N_CEN,)),
            dma((NY,)), dma((NY,)), dma((N_TOK,)), dma((N_TOK,)), dma((NX,)), dma((NX,)),
            dma((NY,)), dma((NY,)), dma((NZ,)), dma((NZ,)),
        ],
        compiler_params=pltpu.CompilerParams(
            collective_id=0, has_side_effects=True, vmem_limit_bytes=VMEM_LIMIT
        ),
    )(tokens, nearest.reshape(1, ROWS), centroids, log_prior.reshape(LOCAL // ROWS, ROWS))
    upd, norm, res = pl.pallas_call(
        hand_on,
        out_shape=tuple(jax.ShapeDtypeStruct(v.shape, v.dtype) for v in (upd, norm, res)),
        in_specs=[pl.BlockSpec(memory_space=pltpu.VMEM)] * 3,
        out_specs=(pl.BlockSpec(memory_space=pltpu.VMEM),) * 3,
        compiler_params=pltpu.CompilerParams(vmem_limit_bytes=VMEM_LIMIT),
    )(upd, norm, res)
    return upd, norm.reshape(ROWS), res


def solution(mesh):
    return jax.shard_map(
        per_device,
        mesh=mesh,
        in_specs=(P("tok", None), P("tok"), P(("tok", "cen"), None), P(("tok", "cen"))),
        out_specs=(P(("tok", "cen"), None), P("tok"), P(("tok", "cen"), None)),
        check_vma=False,
    )
```

```python
import functools
import math

import jax
import jax.numpy as jnp
from jax import lax
from jax.experimental import pallas as pl
from jax.experimental.pallas import tpu as pltpu
from jax.sharding import PartitionSpec as P

MESH = pl.DeviceIdType.MESH
NX, NY, NZ = 4, 8, 8
N_TOK, N_CEN = 32, 16
ROWS = 128
WIDTH = 128
LOCAL = 1024
CHUNK = 256
LN2 = math.log(2.0)
VMEM_LIMIT = 60 << 20
PICK_B, PICK_A = 8, 8
SPLIT = 1


def div(a, b):
    return a // b if isinstance(a, int) else lax.div(a, b)


def rem(a, b):
    return a % b if isinstance(a, int) else lax.rem(a, b)


def ring(s):
    return div(s + 1, 2) * (2 * rem(s, 2) - 1)


def place(d):
    far = div(d, 5)
    return (1 - far) * (2 * d - div(d + 7, 8)) + far * (16 - 2 * d)


def loop(lo, hi, body):
    def step(i, carry):
        body(i)
        return carry

    lax.fori_loop(lo, hi, step, 0)


def each(lo, hi, body):
    for i in range(lo, hi):
        body(i)


def split3(v):
    hi = v.astype(jnp.bfloat16).astype(jnp.float32)
    mid = (v - hi).astype(jnp.bfloat16).astype(jnp.float32)
    return hi, mid, v - hi - mid


def kernel(
    tok_hbm, ids_hbm, cen_hbm, lp_hbm, upd_ref, norm_ref, res_ref,
    tok_all, ids_all, cen2, lp_ref, cen_aug, tok_t, e_ref, g_ref, acc, m_ref, l_send, l_cen, l_tok, l_all,
    cols, ya_out, ya_in, ta_out, ta_in, xb_out, xb_in, yb_out, yb_in, zb_out, zb_in, tok_f32,
    in_s, z_s, z_r, x_s, x_r, f_s, f_r, idz_s, idz_r, idx_s, idx_r, cen_s, cen_r,
    lc_s, lc_r, lt_s, lt_r, la_s, la_r, ya_s, ya_r, ta_s, ta_r, xb_s, xb_r, yb_s, yb_r, zb_s, zb_r,
):
    t = lax.axis_index("tok")
    n = lax.axis_index("cen")
    x, z = rem(t, NX), div(t, NX)
    y, c = div(n, 2), rem(n, 2)
    sib = (t, y * 2 + 1 - c)
    unit = math.log2(math.e) / math.sqrt(WIDTH)

    def at_x(k):
        return (z * NX + rem(x + k, NX), n)

    def at_y(k):
        return (t, rem(y + k, NY) * 2 + c)

    def at_z(k):
        return (rem(z + k, NZ) * NX + x, n)

    def copy(src, dst, send, recv, dev):
        return pltpu.make_async_remote_copy(
            src_ref=src, dst_ref=dst, send_sem=send, recv_sem=recv, device_id=dev, device_id_type=MESH
        )

    barrier = pltpu.get_barrier_semaphore()

    def greet(dev):
        pl.semaphore_signal(barrier, inc=1, device_id=dev, device_id_type=MESH)

    each(1, NZ, lambda k: greet(at_z(k)))
    each(1, NY, lambda k: greet(at_y(k)))
    each(1, NX, lambda k: greet(at_x(k)))
    greet(sib)

    fetch = [
        pltpu.make_async_copy(tok_hbm, tok_all.at[t], in_s.at[0]),
        pltpu.make_async_copy(ids_hbm, ids_all.at[x * NZ + z], in_s.at[1]),
        pltpu.make_async_copy(cen_hbm, cen2.at[c], in_s.at[2]),
        pltpu.make_async_copy(lp_hbm, lp_ref, in_s.at[3]),
    ]
    for f in fetch:
        f.start()
    for f in fetch:
        f.wait()
    tok_f32[...] = tok_all[pl.ds(t, 1)][0].astype(jnp.float32)
    lane = lax.broadcasted_iota(jnp.int32, (ROWS, WIDTH), 1)
    lp_cols = jnp.transpose(lp_ref[...] * math.sqrt(WIDTH))
    for a in range(LOCAL // ROWS):
        hi, mid, low = split3(lp_cols[:, a : a + 1])
        extra = jnp.where(lane == 0, hi, jnp.where(lane == 1, mid, jnp.where(lane == 2, low, 0.0)))
        cen_aug[a * ROWS : (a + 1) * ROWS, WIDTH:] = extra.astype(jnp.bfloat16)
    cen_aug[:LOCAL, :WIDTH] = cen2[pl.ds(c, 1)][0]
    eye = lane == lax.broadcasted_iota(jnp.int32, (ROWS, WIDTH), 0)
    cen_aug[LOCAL:, :WIDTH] = jnp.where(eye, 1.0, 0.0).astype(jnp.bfloat16)
    cen_aug[LOCAL:, WIDTH:] = jnp.zeros((WIDTH, WIDTH), jnp.bfloat16)

    pl.semaphore_wait(barrier, NZ - 1 + NY - 1 + NX - 1 + 1)

    def idz_copy(k):
        return copy(ids_all.at[x * NZ + z], ids_all.at[x * NZ + z], idz_s.at[k], idz_r.at[k], at_z(k))

    def idx_copy(k):
        rows = pl.ds(x * NZ, NZ)
        return copy(ids_all.at[rows], ids_all.at[rows], idx_s.at[k], idx_r.at[k], at_x(k))

    def cen_copy():
        return copy(cen2.at[c], cen2.at[c], cen_s, cen_r, sib)

    def z_copy(s):
        return copy(tok_all.at[t], tok_all.at[t], z_s.at[s], z_r.at[s], at_z(NZ - ring(s)))

    def block(s, k):
        return rem(z + ring(s) + NZ, NZ) * NX + rem(x + k, NX)

    def x_copy(s, k):
        b = block(s, 0)
        return copy(tok_all.at[b], tok_all.at[b], x_s.at[s, k], x_r.at[s, k], at_x(NX - k))

    def f_copy(s, k):
        b = block(s, k)
        return copy(tok_all.at[b], tok_all.at[b], f_s.at[s, k], f_r.at[s, k], sib)

    def if_mine(s, core, todo):
        pl.when(rem(s, 2) == core)(todo)

    each(1, NZ, lambda k: idz_copy(k).start())
    each(1, NZ, lambda s: if_mine(s, c, lambda: z_copy(s).start()))
    cen_copy().start()

    def receive_z(s):
        def todo():
            @pl.when(s > 0)
            def _():
                z_copy(s).wait_recv()

            for k in range(1, NX):
                x_copy(s, k).start()

            @pl.when(s > 0)
            def _():
                f_copy(s, 0).start()

        if_mine(s, c, todo)

    def receive_x(s):
        def todo():
            for k in range(1, NX):
                x_copy(s, k).wait_recv()
                f_copy(s, k).start()

        if_mine(s, c, todo)

    ones = jnp.where(lax.broadcasted_iota(jnp.int32, (CHUNK, WIDTH), 1) < 3, 1.0, 0.0).astype(jnp.bfloat16)

    def lc_copy(ch):
        return copy(l_send.at[ch], l_cen.at[n], lc_s.at[ch], lc_r.at[n], (t, ch))

    def score(s):
        def todo():
            @pl.when(s > 0)
            def _():
                f_copy(s, 0).wait_recv()

            for k in range(1, NX):
                f_copy(s, k).wait_recv()

        if_mine(s, 1 - c, todo)
        zz = rem(z + ring(s) + NZ, NZ)
        spot = place(rem(zz - y + NY, NY))
        parts = []
        for h in range(2):
            ch = 2 * zz + h
            tk = tok_all[pl.ds(2 * ch, 2)].reshape(CHUNK, WIDTH)
            raw = lax.dot_general(
                cen_aug[...], jnp.concatenate([tk, ones], axis=1),
                (((1,), (1,)), ((), ())), preferred_element_type=jnp.float32,
            )
            tok_t[pl.ds(ch, 1)] = raw[LOCAL:].astype(jnp.bfloat16)[None]
            raw = raw[:LOCAL]
            top = jnp.max(raw, axis=0, keepdims=True)
            e = jnp.exp2((raw - top) * unit)
            e_ref[:, pl.ds(pl.multiple_of((2 * spot + h) * CHUNK, CHUNK), CHUNK)] = e.astype(jnp.bfloat16)
            total = jnp.sum(e, axis=0, keepdims=True)
            m_ref[pl.ds(ch, 1)] = (top * unit)[None]
            part = top * unit + jnp.log2(total)
            l_send[pl.ds(ch, 1)] = part[None]
            parts.append(part)
        for h in range(2):
            ch = 2 * zz + h
            part = parts[h]

            @pl.when(ch != n)
            def _():
                lc_copy(ch).start()

            @pl.when(ch == n)
            def _():
                l_cen[pl.ds(ch, 1)] = part[None]

    def ya_copy(k):
        return copy(ya_out.at[rem(y + k, NY)], ya_in.at[k], ya_s.at[k], ya_r.at[k], at_y(k))

    def xb_copy(k):
        return copy(xb_out.at[rem(x + k, NX)], xb_in.at[k], xb_s.at[k], xb_r.at[k], at_x(k))

    def yb_copy(k):
        return copy(yb_out.at[rem(y + k, NY)], yb_in.at[k], yb_s.at[k], yb_r.at[k], at_y(k))

    def pick_prepare():
        each(1, NX, lambda k: idx_copy(k).wait_recv())
        first = (t * N_CEN + y * 2) * LOCAL
        rel = (ids_all[...].reshape(N_TOK, ROWS) - first).astype(jnp.float32)
        rel = jnp.transpose(rel).reshape(NY, 2, 8, N_TOK)
        rel = jnp.where(c == 0, rel[:, 0], rel[:, 1]).reshape(NY * 8, N_TOK)

        def spread(zb, xb):
            i = xb * NZ + zb
            return jnp.broadcast_to(rel[:, i : i + 1], (NY * 8, WIDTH)).reshape(NY, 1, 8, WIDTH)

        for p in range(N_TOK // 2):
            if p < 8:
                one, two = (p // 2, (2 * p) % NX), (p // 2, (2 * p) % NX + 1)
            else:
                one, two = (2 * (p // 4), p % NX), (2 * (p // 4) + 1, p % NX)
            cols[p] = jnp.concatenate([spread(*one), spread(*two)], axis=1).reshape(ROWS, WIDTH)

    def part(g):
        at = lax.broadcasted_iota(jnp.int32, (1, WIDTH), 1).astype(jnp.float32)
        want = cols[pl.ds(4 * g, 4)].reshape(4 * ROWS, WIDTH)
        hot = jnp.concatenate(
            [jnp.where(want == at + float(WIDTH * b), 1.0, 0.0).astype(jnp.bfloat16) for b in range(2 * LOCAL // WIDTH)],
            axis=1,
        )
        got = jnp.dot(hot, cen2[...].reshape(2 * LOCAL, WIDTH), preferred_element_type=jnp.float32)
        return got.astype(jnp.bfloat16).reshape(4, NY, 16, WIDTH)

    def part_a(g):
        got = part(g)
        for k in range(4):
            ya_out[:, pl.ds(pl.multiple_of((4 * g + k) * 16, 16), 16), :] = got[k]

    def part_b(g):
        got = part(g)
        for k in range(4):
            xb_out[k, :, pl.ds(pl.multiple_of((g - 2) * 16, 16), 16), :] = got[k]

    def pick_a():
        loop(0, 2, part_a)
        each(1, NY, lambda k: ya_copy(k).start())

    def pick_b():
        pick_prepare()
        loop(2, 4, part_b)
        each(1, NX, lambda k: xb_copy(k).start())

    def ids_along_x():
        each(1, NZ, lambda k: idz_copy(k).wait_recv())
        each(1, NX, lambda k: idx_copy(k).start())

    receive_z(0)
    cen_copy().wait_recv()
    each(1, 3, receive_z)
    receive_x(0)
    each(3, 5, receive_z)
    ids_along_x()

    def step(s):
        @pl.when(s == 1)
        def _():
            each(5, NZ, receive_z)
            each(1, 3, receive_x)

        @pl.when((s >= 1) & (s + 2 < NZ))
        def _():
            receive_x(s + 2)

        if PICK_B < NZ:
            pl.when(s == PICK_B)(pick_b)
        if PICK_A < NZ:
            pl.when(s == PICK_A)(pick_a)
        score(s)

    loop(0, NZ, step)
    if PICK_B >= NZ:
        pick_b()
    if PICK_A >= NZ:
        pick_a()

    def tok_of(j):
        return rem(z + ring(7 - div(j, NX)) + NZ, NZ) * NX + rem(x + 1 + rem(j, NX), NX)

    def cen_of(j):
        return rem(y + ring(7 - div(j, 2)) + NY, NY) * 2 + rem(c + 1 + rem(j, 2), 2)

    def lse(v):
        top = jnp.max(v, axis=0)
        return top + jnp.log2(jnp.sum(jnp.exp2(v - top[None]), axis=0))

    def lc_wait(j):
        src = cen_of(j)
        copy(l_send.at[src], l_cen.at[src], lc_s.at[src], lc_r.at[src], (t, src)).wait_recv()

    def lt_copy(to):
        return copy(l_tok.at[t], l_tok.at[t], lt_s.at[to], lt_r.at[t], (to, n))

    def lt_wait(j):
        src = tok_of(j)
        copy(l_tok.at[src], l_tok.at[src], lt_s.at[src], lt_r.at[src], (src, n)).wait_recv()

    def la_copy(to):
        return copy(l_all.at[n], l_all.at[n], la_s.at[to], la_r.at[n], (t, to))

    def la_wait(src):
        copy(l_all.at[src], l_all.at[src], la_s.at[src], la_r.at[src], (t, src)).wait_recv()

    def ta_copy(to):
        return copy(ta_out.at[to], ta_in.at[t], ta_s.at[to], ta_r.at[t], (to, n))

    def ta_wait(src):
        copy(ta_out.at[0], ta_in.at[src], ta_s.at[0], ta_r.at[src], (src, n)).wait_recv()

    half = NZ // 2

    def zb_copy(zt):
        dev = (zt * NX + x, n)
        return copy(zb_out.at[zt - half], zb_in.at[z], zb_s.at[zt], zb_r.at[z], dev)

    def zb_wait(src):
        copy(zb_out.at[0], zb_in.at[src], zb_s.at[0], zb_r.at[src], (src * NX + x, n)).wait_recv()

    each(0, N_CEN - 1, lc_wait)
    l_tok[pl.ds(t, 1)] = lse(l_cen[...])[None]
    each(0, N_TOK - 1, lambda j: lt_copy(tok_of(j)).start())

    each(1, NX, lambda k: xb_copy(k).wait_recv())
    rows = xb_out[pl.ds(x, 1)][0].astype(jnp.float32)
    for k in range(1, NX):
        rows = rows + xb_in[k].astype(jnp.float32)
    yb_out[...] = rows.astype(jnp.bfloat16)
    each(1, NY, lambda k: yb_copy(k).start())

    def sent(s):
        def todo():
            if s > 0:
                z_copy(s).wait_send()
                f_copy(s, 0).wait_send()
            for k in range(1, NX):
                x_copy(s, k).wait_send()
                f_copy(s, k).wait_send()

        if_mine(s, c, todo)

    each(0, NZ, sent)
    cen_copy().wait_send()
    each(1, NZ, lambda k: idz_copy(k).wait_send())
    each(1, NX, lambda k: idx_copy(k).wait_send())
    each(0, N_CEN - 1, lambda j: lc_copy(cen_of(j)).wait_send())

    each(0, N_TOK - 1, lt_wait)
    l_all[pl.ds(n, 1)] = lse(l_tok[...])[None]
    each(0, N_CEN - 1, lambda j: la_copy(cen_of(j)).start())

    each(1, NY, lambda k: ya_copy(k).wait_recv())
    rows = ya_out[pl.ds(y, 1)][0].astype(jnp.float32)
    for k in range(1, NY):
        rows = rows + ya_in[k].astype(jnp.float32)
    ta_out[...] = rows.reshape(half * NX, 8, WIDTH)

    def ta_each(act):
        def body(to):
            @pl.when(to != t)
            def _():
                act(to)

        each(0, half * NX, body)

    ta_each(lambda to: ta_copy(to).start())

    each(1, NY, lambda k: yb_copy(k).wait_recv())
    rows = yb_out[pl.ds(y, 1)][0].astype(jnp.float32)
    for k in range(1, NY):
        rows = rows + yb_in[k].astype(jnp.float32)
    zb_out[...] = rows.reshape(half, 8, WIDTH)

    def zb_each(act):
        def body(zt):
            @pl.when(zt != z)
            def _():
                act(zt)

        each(half, NZ, body)

    zb_each(lambda zt: zb_copy(zt).start())

    each(1, NX, lambda k: xb_copy(k).wait_send())
    each(1, NY, lambda k: ya_copy(k).wait_send())
    each(0, N_TOK - 1, lambda j: lt_copy(tok_of(j)).wait_send())

    upper = lax.broadcasted_iota(jnp.int32, (WIDTH, CHUNK), 0) < 64

    def scale(k):
        yy = rem(y + ring(k) + NY, NY)
        for h in range(2):
            ch = 2 * yy + h

            @pl.when(ch != n)
            def _():
                la_wait(ch)

            g = jnp.exp2(m_ref[pl.ds(ch, 1)][0] - l_all[pl.ds(ch, 1)][0])
            g_hi = g.astype(jnp.bfloat16).astype(jnp.float32)
            top = tok_t[pl.ds(ch, 1)][0].astype(jnp.float32) * g
            low = jnp.where(upper, g_hi, g - g_hi)
            at = (2 * k + h) * CHUNK
            g_ref[:WIDTH, at : at + CHUNK] = top.astype(jnp.bfloat16)
            g_ref[WIDTH:, at : at + CHUNK] = low.astype(jnp.bfloat16)

    def product(lo, hi):
        at = slice(lo * 2 * CHUNK, hi * 2 * CHUNK)
        return lax.dot_general(
            e_ref[:, at], g_ref[:, at], (((1,), (1,)), ((), ())), preferred_element_type=jnp.float32
        )

    for k in range(SPLIT):
        scale(k)
    acc[...] = product(0, SPLIT)
    for k in range(SPLIT, NY):
        scale(k)
    acc[...] += product(SPLIT, NY)
    mass = acc[:, WIDTH:]
    mass = mass + pltpu.roll(mass, 64, 1)
    upd_ref[...] = (acc[:, :WIDTH] / mass).astype(jnp.bfloat16)

    own = l_all[pl.ds(div(t, 2), 1)][0] * LN2
    norm_ref[...] = jnp.where(rem(t, 2) == 0, own[:, :ROWS], own[:, ROWS:])

    mine = tok_f32[pl.ds(pl.multiple_of(n * 8, 8), 8), :]

    @pl.when(z < half)
    def _():
        ta_in[pl.ds(t, 1)] = ta_out[pl.ds(t, 1)]
        each(0, N_TOK - 1, lambda j: ta_wait(tok_of(j)))
        res_ref[...] = (mine - jnp.sum(ta_in[...], axis=0)).astype(jnp.bfloat16)

    @pl.when(z >= half)
    def _():
        zb_in[pl.ds(z, 1)] = zb_out[pl.ds(z - half, 1)]
        each(1, NZ, lambda k: zb_wait(rem(z + k, NZ)))
        res_ref[...] = (mine - jnp.sum(zb_in[...], axis=0)).astype(jnp.bfloat16)

    each(1, NY, lambda k: yb_copy(k).wait_send())
    each(0, N_CEN - 1, lambda j: la_copy(cen_of(j)).wait_send())
    ta_each(lambda to: ta_copy(to).wait_send())
    zb_each(lambda zt: zb_copy(zt).wait_send())


def hand_on(upd_in, norm_in, res_in, upd_ref, norm_ref, res_ref):
    upd_ref[...] = upd_in[...]
    norm_ref[...] = norm_in[...]
    res_ref[...] = res_in[...]


def per_device(tokens, nearest, centroids, log_prior):
    bf, f32, dma, vmem = jnp.bfloat16, jnp.float32, pltpu.SemaphoreType.DMA, pltpu.VMEM
    upd, norm, res = pl.pallas_call(
        kernel,
        out_shape=(
            jax.ShapeDtypeStruct((LOCAL, WIDTH), bf),
            jax.ShapeDtypeStruct((1, ROWS), f32),
            jax.ShapeDtypeStruct((8, WIDTH), bf),
        ),
        in_specs=[pl.BlockSpec(memory_space=pltpu.HBM)] * 4,
        out_specs=(pl.BlockSpec(memory_space=pltpu.VMEM),) * 3,
        scratch_shapes=[
            vmem((N_TOK, ROWS, WIDTH), bf),
            vmem((N_TOK, 1, ROWS), jnp.int32),
            vmem((2, LOCAL, WIDTH), bf),
            vmem((LOCAL // ROWS, ROWS), f32),
            vmem((LOCAL + WIDTH, 2 * WIDTH), bf),
            vmem((N_CEN, WIDTH, CHUNK), bf),
            vmem((LOCAL, N_TOK * ROWS), bf),
            vmem((2 * WIDTH, N_TOK * ROWS), bf),
            vmem((LOCAL, 2 * WIDTH), f32),
            vmem((N_CEN, 1, CHUNK), f32),
            vmem((N_CEN, 1, CHUNK), f32),
            vmem((N_CEN, 1, CHUNK), f32),
            vmem((N_TOK, 1, CHUNK), f32),
            vmem((N_CEN, 1, CHUNK), f32),
            vmem((N_TOK // 2, ROWS, WIDTH), f32),
            vmem((NY, ROWS, WIDTH), bf), vmem((NY, ROWS, WIDTH), bf),
            vmem((N_TOK // 2, 8, WIDTH), f32), vmem((N_TOK, 8, WIDTH), f32),
            vmem((NX, NY, 32, WIDTH), bf), vmem((NX, NY, 32, WIDTH), bf),
            vmem((NY, 32, WIDTH), bf), vmem((NY, 32, WIDTH), bf),
            vmem((NZ // 2, 8, WIDTH), f32), vmem((NZ, 8, WIDTH), f32),
            vmem((ROWS, WIDTH), f32),
            dma((4,)), dma((NZ,)), dma((NZ,)), dma((NZ, NX)), dma((NZ, NX)), dma((NZ, NX)), dma((NZ, NX)),
            dma((NZ,)), dma((NZ,)), dma((NX,)), dma((NX,)), dma, dma,
            dma((N_CEN,)), dma((N_CEN,)), dma((N_TOK,)), dma((N_TOK,)), dma((N_CEN,)), dma((N_CEN,)),
            dma((NY,)), dma((NY,)), dma((N_TOK,)), dma((N_TOK,)), dma((NX,)), dma((NX,)),
            dma((NY,)), dma((NY,)), dma((NZ,)), dma((NZ,)),
        ],
        compiler_params=pltpu.CompilerParams(
            collective_id=0, has_side_effects=True, vmem_limit_bytes=VMEM_LIMIT
        ),
    )(tokens, nearest.reshape(1, ROWS), centroids, log_prior.reshape(LOCAL // ROWS, ROWS))
    upd, norm, res = pl.pallas_call(
        hand_on,
        out_shape=tuple(jax.ShapeDtypeStruct(v.shape, v.dtype) for v in (upd, norm, res)),
        in_specs=[pl.BlockSpec(memory_space=pltpu.VMEM)] * 3,
        out_specs=(pl.BlockSpec(memory_space=pltpu.VMEM),) * 3,
        compiler_params=pltpu.CompilerParams(vmem_limit_bytes=VMEM_LIMIT),
    )(upd, norm, res)
    return upd, norm.reshape(ROWS), res


def solution(mesh):
    return jax.shard_map(
        per_device,
        mesh=mesh,
        in_specs=(P("tok", None), P("tok"), P(("tok", "cen"), None), P(("tok", "cen"))),
        out_specs=(P(("tok", "cen"), None), P("tok"), P(("tok", "cen"), None)),
        check_vma=False,
    )
```

```python
import functools
import math

import jax
import jax.numpy as jnp
from jax import lax
from jax.experimental import pallas as pl
from jax.experimental.pallas import tpu as pltpu
from jax.sharding import PartitionSpec as P

MESH = pl.DeviceIdType.MESH
NX, NY, NZ = 4, 8, 8
N_TOK, N_CEN = 32, 16
ROWS = 128
WIDTH = 128
LOCAL = 1024
CHUNK = 256
LN2 = math.log(2.0)
VMEM_LIMIT = 60 << 20
PICK_B, PICK_A = 8, 8
SPLIT = 1


def div(a, b):
    return a // b if isinstance(a, int) else lax.div(a, b)


def rem(a, b):
    return a % b if isinstance(a, int) else lax.rem(a, b)


def ring(s):
    return div(s + 1, 2) * (2 * rem(s, 2) - 1)


def place(d):
    far = div(d, 5)
    return (1 - far) * (2 * d - div(d + 7, 8)) + far * (16 - 2 * d)


def loop(lo, hi, body):
    def step(i, carry):
        body(i)
        return carry

    lax.fori_loop(lo, hi, step, 0)


def each(lo, hi, body):
    for i in range(lo, hi):
        body(i)


def split3(v):
    hi = v.astype(jnp.bfloat16).astype(jnp.float32)
    mid = (v - hi).astype(jnp.bfloat16).astype(jnp.float32)
    return hi, mid, v - hi - mid


def kernel(
    tok_hbm, ids_hbm, cen_hbm, lp_hbm, upd_ref, norm_ref, res_ref,
    tok_all, ids_all, cen2, lp_ref, cen_aug, tok_t, e_ref, g_ref, acc, m_ref, l_send, l_cen, l_tok, l_all,
    cols, ya_out, ya_in, ta_out, ta_in, xb_out, xb_in, yb_out, yb_in, zb_out, zb_in, tok_f32,
    in_s, z_s, z_r, x_s, x_r, f_s, f_r, idz_s, idz_r, idx_s, idx_r, cen_s, cen_r,
    lc_s, lc_r, lt_s, lt_r, la_s, la_r, ya_s, ya_r, ta_s, ta_r, xb_s, xb_r, yb_s, yb_r, zb_s, zb_r,
):
    t = lax.axis_index("tok")
    n = lax.axis_index("cen")
    x, z = rem(t, NX), div(t, NX)
    y, c = div(n, 2), rem(n, 2)
    sib = (t, y * 2 + 1 - c)
    unit = math.log2(math.e) / math.sqrt(WIDTH)

    def at_x(k):
        return (z * NX + rem(x + k, NX), n)

    def at_y(k):
        return (t, rem(y + k, NY) * 2 + c)

    def at_z(k):
        return (rem(z + k, NZ) * NX + x, n)

    def copy(src, dst, send, recv, dev):
        return pltpu.make_async_remote_copy(
            src_ref=src, dst_ref=dst, send_sem=send, recv_sem=recv, device_id=dev, device_id_type=MESH
        )

    barrier = pltpu.get_barrier_semaphore()

    def greet(dev):
        pl.semaphore_signal(barrier, inc=1, device_id=dev, device_id_type=MESH)

    each(1, NZ, lambda k: greet(at_z(k)))
    each(1, NY, lambda k: greet(at_y(k)))
    each(1, NX, lambda k: greet(at_x(k)))
    greet(sib)

    fetch = [
        pltpu.make_async_copy(tok_hbm, tok_all.at[t], in_s.at[0]),
        pltpu.make_async_copy(ids_hbm, ids_all.at[x * NZ + z], in_s.at[1]),
        pltpu.make_async_copy(cen_hbm, cen2.at[c], in_s.at[2]),
        pltpu.make_async_copy(lp_hbm, lp_ref, in_s.at[3]),
    ]
    for f in fetch:
        f.start()
    for f in fetch:
        f.wait()
    tok_f32[...] = tok_all[pl.ds(t, 1)][0].astype(jnp.float32)
    lane = lax.broadcasted_iota(jnp.int32, (ROWS, WIDTH), 1)
    lp_cols = jnp.transpose(lp_ref[...] * math.sqrt(WIDTH))
    for a in range(LOCAL // ROWS):
        hi, mid, low = split3(lp_cols[:, a : a + 1])
        extra = jnp.where(lane == 0, hi, jnp.where(lane == 1, mid, jnp.where(lane == 2, low, 0.0)))
        cen_aug[a * ROWS : (a + 1) * ROWS, WIDTH:] = extra.astype(jnp.bfloat16)
    cen_aug[:LOCAL, :WIDTH] = cen2[pl.ds(c, 1)][0]
    eye = lane == lax.broadcasted_iota(jnp.int32, (ROWS, WIDTH), 0)
    cen_aug[LOCAL:, :WIDTH] = jnp.where(eye, 1.0, 0.0).astype(jnp.bfloat16)
    cen_aug[LOCAL:, WIDTH:] = jnp.zeros((WIDTH, WIDTH), jnp.bfloat16)

    pl.semaphore_wait(barrier, NZ - 1 + NY - 1 + NX - 1 + 1)

    def idz_copy(k):
        return copy(ids_all.at[x * NZ + z], ids_all.at[x * NZ + z], idz_s.at[k], idz_r.at[k], at_z(k))

    def idx_copy(k):
        rows = pl.ds(x * NZ, NZ)
        return copy(ids_all.at[rows], ids_all.at[rows], idx_s.at[k], idx_r.at[k], at_x(k))

    def cen_copy():
        return copy(cen2.at[c], cen2.at[c], cen_s, cen_r, sib)

    def z_copy(s):
        return copy(tok_all.at[t], tok_all.at[t], z_s.at[s], z_r.at[s], at_z(NZ - ring(s)))

    def block(s, k):
        return rem(z + ring(s) + NZ, NZ) * NX + rem(x + k, NX)

    def x_copy(s, k):
        b = block(s, 0)
        return copy(tok_all.at[b], tok_all.at[b], x_s.at[s, k], x_r.at[s, k], at_x(NX - k))

    def f_copy(s, k):
        b = block(s, k)
        return copy(tok_all.at[b], tok_all.at[b], f_s.at[s, k], f_r.at[s, k], sib)

    def if_mine(s, core, todo):
        pl.when(rem(s, 2) == core)(todo)

    each(1, NZ, lambda k: idz_copy(k).start())
    each(1, NZ, lambda s: if_mine(s, c, lambda: z_copy(s).start()))
    cen_copy().start()

    def receive_z(s):
        def todo():
            @pl.when(s > 0)
            def _():
                z_copy(s).wait_recv()

            for k in range(1, NX):
                x_copy(s, k).start()

            @pl.when(s > 0)
            def _():
                f_copy(s, 0).start()

        if_mine(s, c, todo)

    def receive_x(s):
        def todo():
            for k in range(1, NX):
                x_copy(s, k).wait_recv()
                f_copy(s, k).start()

        if_mine(s, c, todo)

    ones = jnp.where(lax.broadcasted_iota(jnp.int32, (CHUNK, WIDTH), 1) < 3, 1.0, 0.0).astype(jnp.bfloat16)

    def lc_copy(ch):
        return copy(l_send.at[ch], l_cen.at[n], lc_s.at[ch], lc_r.at[n], (t, ch))

    def score(s):
        def todo():
            @pl.when(s > 0)
            def _():
                f_copy(s, 0).wait_recv()

            for k in range(1, NX):
                f_copy(s, k).wait_recv()

        if_mine(s, 1 - c, todo)
        zz = rem(z + ring(s) + NZ, NZ)
        spot = place(rem(zz - y + NY, NY))
        parts = []
        for h in range(2):
            ch = 2 * zz + h
            tk = tok_all[pl.ds(2 * ch, 2)].reshape(CHUNK, WIDTH)
            raw = lax.dot_general(
                cen_aug[...], jnp.concatenate([tk, ones], axis=1),
                (((1,), (1,)), ((), ())), preferred_element_type=jnp.float32,
            )
            tok_t[pl.ds(ch, 1)] = raw[LOCAL:].astype(jnp.bfloat16)[None]
            raw = raw[:LOCAL]
            top = jnp.max(raw, axis=0, keepdims=True)
            e = jnp.exp2((raw - top) * unit)
            e_ref[:, pl.ds(pl.multiple_of((2 * spot + h) * CHUNK, CHUNK), CHUNK)] = e.astype(jnp.bfloat16)
            total = jnp.sum(e, axis=0, keepdims=True)
            m_ref[pl.ds(ch, 1)] = (top * unit)[None]
            part = top * unit + jnp.log2(total)
            l_send[pl.ds(ch, 1)] = part[None]
            parts.append(part)
        for h in range(2):
            ch = 2 * zz + h
            part = parts[h]

            @pl.when(ch != n)
            def _():
                lc_copy(ch).start()

            @pl.when(ch == n)
            def _():
                l_cen[pl.ds(ch, 1)] = part[None]

    def ya_copy(k):
        return copy(ya_out.at[rem(y + k, NY)], ya_in.at[k], ya_s.at[k], ya_r.at[k], at_y(k))

    def xb_copy(k):
        return copy(xb_out.at[rem(x + k, NX)], xb_in.at[k], xb_s.at[k], xb_r.at[k], at_x(k))

    def yb_copy(k):
        return copy(yb_out.at[rem(y + k, NY)], yb_in.at[k], yb_s.at[k], yb_r.at[k], at_y(k))

    def pick_prepare():
        each(1, NX, lambda k: idx_copy(k).wait_recv())
        first = (t * N_CEN + y * 2) * LOCAL
        rel = (ids_all[...].reshape(N_TOK, ROWS) - first).astype(jnp.float32)
        rel = jnp.transpose(rel).reshape(NY, 2, 8, N_TOK)
        rel = jnp.where(c == 0, rel[:, 0], rel[:, 1]).reshape(NY * 8, N_TOK)

        def spread(zb, xb):
            i = xb * NZ + zb
            return jnp.broadcast_to(rel[:, i : i + 1], (NY * 8, WIDTH)).reshape(NY, 1, 8, WIDTH)

        for p in range(N_TOK // 2):
            if p < 8:
                one, two = (p // 2, (2 * p) % NX), (p // 2, (2 * p) % NX + 1)
            else:
                one, two = (2 * (p // 4), p % NX), (2 * (p // 4) + 1, p % NX)
            cols[p] = jnp.concatenate([spread(*one), spread(*two)], axis=1).reshape(ROWS, WIDTH)

    def part(g):
        at = lax.broadcasted_iota(jnp.int32, (1, WIDTH), 1).astype(jnp.float32)
        want = cols[pl.ds(4 * g, 4)].reshape(4 * ROWS, WIDTH)
        hot = jnp.concatenate(
            [jnp.where(want == at + float(WIDTH * b), 1.0, 0.0).astype(jnp.bfloat16) for b in range(2 * LOCAL // WIDTH)],
            axis=1,
        )
        got = jnp.dot(hot, cen2[...].reshape(2 * LOCAL, WIDTH), preferred_element_type=jnp.float32)
        return got.astype(jnp.bfloat16).reshape(4, NY, 16, WIDTH)

    def part_a(g):
        got = part(g)
        for k in range(4):
            ya_out[:, pl.ds(pl.multiple_of((4 * g + k) * 16, 16), 16), :] = got[k]

    def part_b(g):
        got = part(g)
        for k in range(4):
            xb_out[k, :, pl.ds(pl.multiple_of((g - 2) * 16, 16), 16), :] = got[k]

    def pick_a():
        loop(0, 2, part_a)
        each(1, NY, lambda k: ya_copy(k).start())

    def pick_b():
        pick_prepare()
        pick_b2()

    def pick_b2():
        loop(2, 4, part_b)
        each(1, NX, lambda k: xb_copy(k).start())

    def ids_along_x():
        each(1, NZ, lambda k: idz_copy(k).wait_recv())
        each(1, NX, lambda k: idx_copy(k).start())

    receive_z(0)
    cen_copy().wait_recv()
    each(1, 3, receive_z)
    receive_x(0)
    each(3, 5, receive_z)
    ids_along_x()

    def step(s):
        @pl.when(s == 1)
        def _():
            each(5, NZ, receive_z)
            each(1, 3, receive_x)

        @pl.when((s >= 1) & (s + 2 < NZ))
        def _():
            receive_x(s + 2)

        if PICK_B < NZ:
            pl.when(s == PICK_B)(pick_b)
        if PICK_A < NZ:
            pl.when(s == PICK_A)(pick_a)
        score(s)

    loop(0, NZ, step)
    pick_prepare()
    pick_a()
    pick_b2()

    def tok_of(j):
        return rem(z + ring(7 - div(j, NX)) + NZ, NZ) * NX + rem(x + 1 + rem(j, NX), NX)

    def cen_of(j):
        return rem(y + ring(7 - div(j, 2)) + NY, NY) * 2 + rem(c + 1 + rem(j, 2), 2)

    def lse(v):
        top = jnp.max(v, axis=0)
        return top + jnp.log2(jnp.sum(jnp.exp2(v - top[None]), axis=0))

    def lc_wait(j):
        src = cen_of(j)
        copy(l_send.at[src], l_cen.at[src], lc_s.at[src], lc_r.at[src], (t, src)).wait_recv()

    def lt_copy(to):
        return copy(l_tok.at[t], l_tok.at[t], lt_s.at[to], lt_r.at[t], (to, n))

    def lt_wait(j):
        src = tok_of(j)
        copy(l_tok.at[src], l_tok.at[src], lt_s.at[src], lt_r.at[src], (src, n)).wait_recv()

    def la_copy(to):
        return copy(l_all.at[n], l_all.at[n], la_s.at[to], la_r.at[n], (t, to))

    def la_wait(src):
        copy(l_all.at[src], l_all.at[src], la_s.at[src], la_r.at[src], (t, src)).wait_recv()

    def ta_copy(to):
        return copy(ta_out.at[to], ta_in.at[t], ta_s.at[to], ta_r.at[t], (to, n))

    def ta_wait(src):
        copy(ta_out.at[0], ta_in.at[src], ta_s.at[0], ta_r.at[src], (src, n)).wait_recv()

    half = NZ // 2

    def zb_copy(zt):
        dev = (zt * NX + x, n)
        return copy(zb_out.at[zt - half], zb_in.at[z], zb_s.at[zt], zb_r.at[z], dev)

    def zb_wait(src):
        copy(zb_out.at[0], zb_in.at[src], zb_s.at[0], zb_r.at[src], (src * NX + x, n)).wait_recv()

    each(0, N_CEN - 1, lc_wait)
    l_tok[pl.ds(t, 1)] = lse(l_cen[...])[None]
    each(0, N_TOK - 1, lambda j: lt_copy(tok_of(j)).start())

    each(1, NX, lambda k: xb_copy(k).wait_recv())
    rows = xb_out[pl.ds(x, 1)][0].astype(jnp.float32)
    for k in range(1, NX):
        rows = rows + xb_in[k].astype(jnp.float32)
    yb_out[...] = rows.astype(jnp.bfloat16)
    each(1, NY, lambda k: yb_copy(k).start())

    def sent(s):
        def todo():
            if s > 0:
                z_copy(s).wait_send()
                f_copy(s, 0).wait_send()
            for k in range(1, NX):
                x_copy(s, k).wait_send()
                f_copy(s, k).wait_send()

        if_mine(s, c, todo)

    each(0, NZ, sent)
    cen_copy().wait_send()
    each(1, NZ, lambda k: idz_copy(k).wait_send())
    each(1, NX, lambda k: idx_copy(k).wait_send())
    each(0, N_CEN - 1, lambda j: lc_copy(cen_of(j)).wait_send())

    each(0, N_TOK - 1, lt_wait)
    l_all[pl.ds(n, 1)] = lse(l_tok[...])[None]
    each(0, N_CEN - 1, lambda j: la_copy(cen_of(j)).start())

    each(1, NY, lambda k: ya_copy(k).wait_recv())
    rows = ya_out[pl.ds(y, 1)][0].astype(jnp.float32)
    for k in range(1, NY):
        rows = rows + ya_in[k].astype(jnp.float32)
    ta_out[...] = rows.reshape(half * NX, 8, WIDTH)

    def ta_each(act):
        def body(to):
            @pl.when(to != t)
            def _():
                act(to)

        each(0, half * NX, body)

    ta_each(lambda to: ta_copy(to).start())

    each(1, NY, lambda k: yb_copy(k).wait_recv())
    rows = yb_out[pl.ds(y, 1)][0].astype(jnp.float32)
    for k in range(1, NY):
        rows = rows + yb_in[k].astype(jnp.float32)
    zb_out[...] = rows.reshape(half, 8, WIDTH)

    def zb_each(act):
        def body(zt):
            @pl.when(zt != z)
            def _():
                act(zt)

        each(half, NZ, body)

    zb_each(lambda zt: zb_copy(zt).start())

    each(1, NX, lambda k: xb_copy(k).wait_send())
    each(1, NY, lambda k: ya_copy(k).wait_send())
    each(0, N_TOK - 1, lambda j: lt_copy(tok_of(j)).wait_send())

    upper = lax.broadcasted_iota(jnp.int32, (WIDTH, CHUNK), 0) < 64

    def scale(k):
        yy = rem(y + ring(k) + NY, NY)
        for h in range(2):
            ch = 2 * yy + h

            @pl.when(ch != n)
            def _():
                la_wait(ch)

            g = jnp.exp2(m_ref[pl.ds(ch, 1)][0] - l_all[pl.ds(ch, 1)][0])
            g_hi = g.astype(jnp.bfloat16).astype(jnp.float32)
            top = tok_t[pl.ds(ch, 1)][0].astype(jnp.float32) * g
            low = jnp.where(upper, g_hi, g - g_hi)
            at = (2 * k + h) * CHUNK
            g_ref[:WIDTH, at : at + CHUNK] = top.astype(jnp.bfloat16)
            g_ref[WIDTH:, at : at + CHUNK] = low.astype(jnp.bfloat16)

    def product(lo, hi):
        at = slice(lo * 2 * CHUNK, hi * 2 * CHUNK)
        return lax.dot_general(
            e_ref[:, at], g_ref[:, at], (((1,), (1,)), ((), ())), preferred_element_type=jnp.float32
        )

    for k in range(SPLIT):
        scale(k)
    acc[...] = product(0, SPLIT)
    for k in range(SPLIT, NY):
        scale(k)
    acc[...] += product(SPLIT, NY)
    mass = acc[:, WIDTH:]
    mass = mass + pltpu.roll(mass, 64, 1)
    upd_ref[...] = (acc[:, :WIDTH] / mass).astype(jnp.bfloat16)

    own = l_all[pl.ds(div(t, 2), 1)][0] * LN2
    norm_ref[...] = jnp.where(rem(t, 2) == 0, own[:, :ROWS], own[:, ROWS:])

    mine = tok_f32[pl.ds(pl.multiple_of(n * 8, 8), 8), :]

    @pl.when(z < half)
    def _():
        ta_in[pl.ds(t, 1)] = ta_out[pl.ds(t, 1)]
        each(0, N_TOK - 1, lambda j: ta_wait(tok_of(j)))
        res_ref[...] = (mine - jnp.sum(ta_in[...], axis=0)).astype(jnp.bfloat16)

    @pl.when(z >= half)
    def _():
        zb_in[pl.ds(z, 1)] = zb_out[pl.ds(z - half, 1)]
        each(1, NZ, lambda k: zb_wait(rem(z + k, NZ)))
        res_ref[...] = (mine - jnp.sum(zb_in[...], axis=0)).astype(jnp.bfloat16)

    each(1, NY, lambda k: yb_copy(k).wait_send())
    each(0, N_CEN - 1, lambda j: la_copy(cen_of(j)).wait_send())
    ta_each(lambda to: ta_copy(to).wait_send())
    zb_each(lambda zt: zb_copy(zt).wait_send())


def hand_on(upd_in, norm_in, res_in, upd_ref, norm_ref, res_ref):
    upd_ref[...] = upd_in[...]
    norm_ref[...] = norm_in[...]
    res_ref[...] = res_in[...]


def per_device(tokens, nearest, centroids, log_prior):
    bf, f32, dma, vmem = jnp.bfloat16, jnp.float32, pltpu.SemaphoreType.DMA, pltpu.VMEM
    upd, norm, res = pl.pallas_call(
        kernel,
        out_shape=(
            jax.ShapeDtypeStruct((LOCAL, WIDTH), bf),
            jax.ShapeDtypeStruct((1, ROWS), f32),
            jax.ShapeDtypeStruct((8, WIDTH), bf),
        ),
        in_specs=[pl.BlockSpec(memory_space=pltpu.HBM)] * 4,
        out_specs=(pl.BlockSpec(memory_space=pltpu.VMEM),) * 3,
        scratch_shapes=[
            vmem((N_TOK, ROWS, WIDTH), bf),
            vmem((N_TOK, 1, ROWS), jnp.int32),
            vmem((2, LOCAL, WIDTH), bf),
            vmem((LOCAL // ROWS, ROWS), f32),
            vmem((LOCAL + WIDTH, 2 * WIDTH), bf),
            vmem((N_CEN, WIDTH, CHUNK), bf),
            vmem((LOCAL, N_TOK * ROWS), bf),
            vmem((2 * WIDTH, N_TOK * ROWS), bf),
            vmem((LOCAL, 2 * WIDTH), f32),
            vmem((N_CEN, 1, CHUNK), f32),
            vmem((N_CEN, 1, CHUNK), f32),
            vmem((N_CEN, 1, CHUNK), f32),
            vmem((N_TOK, 1, CHUNK), f32),
            vmem((N_CEN, 1, CHUNK), f32),
            vmem((N_TOK // 2, ROWS, WIDTH), f32),
            vmem((NY, ROWS, WIDTH), bf), vmem((NY, ROWS, WIDTH), bf),
            vmem((N_TOK // 2, 8, WIDTH), f32), vmem((N_TOK, 8, WIDTH), f32),
            vmem((NX, NY, 32, WIDTH), bf), vmem((NX, NY, 32, WIDTH), bf),
            vmem((NY, 32, WIDTH), bf), vmem((NY, 32, WIDTH), bf),
            vmem((NZ // 2, 8, WIDTH), f32), vmem((NZ, 8, WIDTH), f32),
            vmem((ROWS, WIDTH), f32),
            dma((4,)), dma((NZ,)), dma((NZ,)), dma((NZ, NX)), dma((NZ, NX)), dma((NZ, NX)), dma((NZ, NX)),
            dma((NZ,)), dma((NZ,)), dma((NX,)), dma((NX,)), dma, dma,
            dma((N_CEN,)), dma((N_CEN,)), dma((N_TOK,)), dma((N_TOK,)), dma((N_CEN,)), dma((N_CEN,)),
            dma((NY,)), dma((NY,)), dma((N_TOK,)), dma((N_TOK,)), dma((NX,)), dma((NX,)),
            dma((NY,)), dma((NY,)), dma((NZ,)), dma((NZ,)),
        ],
        compiler_params=pltpu.CompilerParams(
            collective_id=0, has_side_effects=True, vmem_limit_bytes=VMEM_LIMIT
        ),
    )(tokens, nearest.reshape(1, ROWS), centroids, log_prior.reshape(LOCAL // ROWS, ROWS))
    upd, norm, res = pl.pallas_call(
        hand_on,
        out_shape=tuple(jax.ShapeDtypeStruct(v.shape, v.dtype) for v in (upd, norm, res)),
        in_specs=[pl.BlockSpec(memory_space=pltpu.VMEM)] * 3,
        out_specs=(pl.BlockSpec(memory_space=pltpu.VMEM),) * 3,
        compiler_params=pltpu.CompilerParams(vmem_limit_bytes=VMEM_LIMIT),
    )(upd, norm, res)
    return upd, norm.reshape(ROWS), res


def solution(mesh):
    return jax.shard_map(
        per_device,
        mesh=mesh,
        in_specs=(P("tok", None), P("tok"), P(("tok", "cen"), None), P(("tok", "cen"))),
        out_specs=(P(("tok", "cen"), None), P("tok"), P(("tok", "cen"), None)),
        check_vma=False,
    )
```
